32 devices in a mesh: ctx: 16 (over z, x, core), head: 2 (over y).
Axes of the slice: x: 2, y: 2, z: 4, core: 2. Of those that a mesh axis runs over, the one named last changes fastest.
Arguments:
- queries: bfloat16 [4096, 8192], P('ctx', 'head'), may hold values from -10 to 10
- key_rows: bfloat16 [4096, 1024], P('ctx', 'head'), may hold values from -4.5 to 4.5
- values: bfloat16 [4096, 1024], P('ctx', 'head'), may hold values from -24 to 24
- lengths: int32 [17], replicated, may hold values from 1 to 2304, as said below
- block_plan: int32 [512], P('ctx'), may hold values from 0 to 511, as said below
- inverse: int32 [512], replicated, may hold values from 0 to 511, as said below
- mask_lo: int32 [512], replicated, may hold values from 0 to 511, as said below
- out_weight: bfloat16 [8192, 4096], P('head'), may hold values from -0.375 to 0.375
Outputs:
- mixed_out: bfloat16 [4096, 4096], P('ctx', 'head')
The draws below stay inside these ranges and needn't reach their ends.
Inputs may be any that keep to these rules, and one draw needn't show every extreme that they name: One document has exactly 2304 tokens, every other is shorter; the lengths sum to 4096. A permutation of the 512 blocks; slot block_plan[b] lies on index block_plan[b] // 32 of ctx; every index receives exactly 32 blocks, and at most 3 blocks of one index go to any one index, which is reached in every draw. inverse[block_plan[b]] == b. mask_lo[b] lies between the block holding the first token of the document of block b's first token and b, both included.
All inputs are finite; a program needn't handle non-finite values.
Results may differ from the reference program's by a relative error of at most 0.02.
Values may be sent and summed in bfloat16 or wider, within the bound.
No kernel may reach another device: no remote copies, remote signals or barrier semaphores. Data moves between devices by JAX's collectives and lax.ppermute only.
A program may use at most 128 MiB of HBM per device.

```python
import jax
import jax.numpy as jnp
from jax import lax

HQ = 64
KVH = 8
HD = 128
D = 4096
BLK = 8
NDOC = 17
TOKENS = 4096
BPD = 32
NBLK = 512
WIN = 64
CAP = 3
MOST = 2304
N_CTX = 16
N_HEAD = 2


def document_lengths(key):
    base_key = jax.random.fold_in(key, 7)
    length_key, order_key = jax.random.split(base_key)
    pair_count = (NDOC - 1) // 2
    half_pair = (TOKENS - MOST) // (2 * pair_count)
    first_half = jax.random.randint(length_key, (pair_count,), 1, 2 * half_pair, dtype=jnp.int32)
    longest = jnp.full((1,), MOST, jnp.int32)
    all_lengths = jnp.concatenate([longest, first_half, 2 * half_pair - first_half])
    order_perm = jax.random.permutation(order_key, NDOC)
    return all_lengths[order_perm].astype(jnp.int32)


def plan_tables(key):
    base_key = jax.random.fold_in(key, 11)
    shift_key, source_key, target_key = jax.random.split(base_key, 3)
    device_count = N_CTX
    per_device = BPD
    lowest = per_device // device_count
    leftover = per_device % device_count
    loads = [lowest + (1 if index < leftover else 0) for index in range(device_count)]
    if max(loads) < CAP:
        loads[0] = loads[0] + 1
        loads[leftover - 1 if leftover > 0 else device_count - 1] = loads[leftover - 1 if leftover > 0 else device_count - 1] - 1
    load_ranks = []
    for index in range(device_count):
        load_ranks = load_ranks + [index] * loads[index]
    rank_table = jnp.array(load_ranks, dtype=jnp.int32)
    shift_ids = jnp.arange(device_count, dtype=jnp.int32)
    drawn_order = jax.random.permutation(shift_key, device_count).astype(jnp.int32)
    priority = jnp.where(shift_ids == device_count // 2, -3, jnp.where(shift_ids == 1, -2, jnp.where(shift_ids == device_count - 1, -1, drawn_order)))
    shift_order = jnp.argsort(priority, stable=True).astype(jnp.int32)
    shift_list = shift_order[rank_table]
    source_perms = jax.vmap(lambda sub_key: jax.random.permutation(sub_key, per_device))(jax.random.split(source_key, device_count)).astype(jnp.int32)
    shifts = shift_list[source_perms]
    source_ids = jnp.arange(device_count, dtype=jnp.int32)[:, None]
    targets = ((source_ids + shifts) % device_count).reshape(-1)
    flat_ids = jnp.arange(device_count * per_device, dtype=jnp.int32)
    same_target = targets[None, :] == targets[:, None]
    earlier = flat_ids[None, :] < flat_ids[:, None]
    arrival = jnp.sum((same_target & earlier).astype(jnp.int32), axis=1)
    slot_perms = jax.vmap(lambda sub_key: jax.random.permutation(sub_key, per_device))(jax.random.split(target_key, device_count)).astype(jnp.int32)
    slots = slot_perms[targets, arrival]
    block_plan = (targets * per_device + slots).astype(jnp.int32)
    inverse = jnp.zeros((device_count * per_device,), jnp.int32).at[block_plan].set(flat_ids)
    return (block_plan, inverse)


def draw_queries(key, part):
    shape_full = (TOKENS, HQ * HD)
    base_draw = jnp.clip(jax.random.normal(jax.random.fold_in(key, 3), shape_full, jnp.float32), -4.5, 4.5)
    return base_draw.astype(jnp.bfloat16)


def draw_key_rows(key, part):
    shape_full = (TOKENS, KVH * HD)
    base_draw = jnp.clip(jax.random.normal(jax.random.fold_in(key, 4), shape_full, jnp.float32), -4.5, 4.5)
    return base_draw.astype(jnp.bfloat16)


def draw_lengths(key, part):
    return document_lengths(key)


def draw_block_plan(key, part):
    return plan_tables(key)[0]


def draw_inverse(key, part):
    return plan_tables(key)[1]


def draw_mask_lo(key, part):
    all_lengths = document_lengths(key)
    doc_ends = jnp.cumsum(all_lengths).astype(jnp.int32)
    doc_starts = doc_ends - all_lengths
    block_ids = jnp.arange(NBLK, dtype=jnp.int32)
    first_rows = block_ids * BLK
    doc_ids = jnp.sum((first_rows[:, None] >= doc_ends[None, :]).astype(jnp.int32), axis=1)
    windows = jax.random.randint(jax.random.fold_in(key, 13), (NDOC,), max(1, WIN // 2), WIN + 1, dtype=jnp.int32)
    windows = jnp.where(all_lengths == MOST, NBLK, windows)
    start_block = jnp.take(doc_starts, doc_ids) // BLK
    return jnp.maximum(start_block, block_ids - jnp.take(windows, doc_ids)).astype(jnp.int32)


def strengthened(values, key, source, target, parts, factor):
    def block_of(dim):
        return (jnp.arange(values.shape[dim]) // (values.shape[dim] // parts)).reshape((-1,) + (1,) * (values.ndim - 1 - dim))

    one_side = jax.random.permutation(key, parts)[block_of(target)]
    other_side = (block_of(target) + parts // 2) % parts
    return jnp.where((block_of(source) == one_side) | (block_of(source) == other_side), factor * values, values)


def level_of(stream_key, dims, shards, least, top_value):
    factor_of = 1.0
    for axis_at, blocks in shards:
        draws = jax.random.uniform(jax.random.fold_in(jax.random.fold_in(stream_key, 6), axis_at), (blocks,), jnp.float32, least / len(shards), top_value / len(shards))
        factor_of = factor_of * jnp.repeat(jnp.exp(draws), dims[axis_at] // blocks).reshape((-1,) + (1,) * (len(dims) - 1 - axis_at))
    return factor_of


def normal_values(rng, dims, width, reach, cuts=(), held_as=jnp.bfloat16):
    values = width * jax.random.normal(rng, dims, jnp.float32)
    if cuts:
        values = values * level_of(rng, dims, cuts, -0.22, 0.18)
    return jnp.clip(values, -reach, reach).astype(held_as)


def bell_draw_with(own_key, shape, width, reach, pieces, heavy, kind=jnp.bfloat16):
    drawn = width * jax.random.normal(own_key, shape, jnp.float32)
    if pieces:
        drawn = drawn * level_of(own_key, shape, pieces, -0.22, 0.18)
    return jnp.clip(strengthened(drawn, jax.random.fold_in(own_key, 3), *heavy), -reach, reach).astype(kind)


def setup_inputs(seed: int = 0) -> dict:
    seeds = jax.random.split(jax.random.key(seed), 9)
    queries = draw_queries(jax.random.fold_in(seeds[8], 71), 0)
    key_rows = draw_key_rows(jax.random.fold_in(seeds[8], 71), 0)
    values = normal_values(seeds[2], (TOKENS, KVH * HD), 4.0, 24.0, ((0, 16), (1, 2)))
    lengths = draw_lengths(jax.random.fold_in(seeds[8], 71), 0)
    block_plan = draw_block_plan(jax.random.fold_in(seeds[8], 71), 0)
    inverse = draw_inverse(jax.random.fold_in(seeds[8], 71), 0)
    mask_lo = draw_mask_lo(jax.random.fold_in(seeds[8], 71), 0)
    out_weight = bell_draw_with(seeds[7], (HQ * HD, D), (HQ * HD // 16) ** -0.5, 0.375, ((0, 2),), (0, 1, 2, 2.0))
    return dict(queries=queries, key_rows=key_rows, values=values, lengths=lengths, block_plan=block_plan, inverse=inverse, mask_lo=mask_lo, out_weight=out_weight)


def document_of(positions, lengths):
    doc_ends = jnp.cumsum(lengths).astype(jnp.int32)
    return jnp.sum((positions[:, None] >= doc_ends[None, :]).astype(jnp.int32), axis=1)


def reference(queries, key_rows, values, lengths, block_plan, inverse, mask_lo, out_weight):
    query_width = HQ * HD
    group_size = HQ // KVH

    def place(source_rows):
        blocked = source_rows.reshape(NBLK, BLK, source_rows.shape[1])
        return jnp.zeros_like(blocked).at[block_plan].set(blocked).reshape(source_rows.shape)

    held_queries = place(queries)
    held_keys = place(key_rows)
    held_values = place(values)
    offsets = jnp.arange(BLK, dtype=jnp.int32)
    held_pos = (inverse[:, None].astype(jnp.int32) * BLK + offsets[None, :]).reshape(TOKENS)
    held_doc = document_of(held_pos, lengths)
    held_lo = jnp.repeat(mask_lo[inverse].astype(jnp.int32), BLK)
    key_block = held_pos // BLK
    query_block = 512 if TOKENS % 512 == 0 else TOKENS
    block_total = TOKENS // query_block
    score_scale = HD ** -0.5
    zero_index = jnp.zeros((), jnp.int32)

    def one_item(item_index):
        group_index = (item_index // block_total).astype(jnp.int32)
        block_index = (item_index % block_total).astype(jnp.int32)
        first_row = (block_index * query_block).astype(jnp.int32)
        query_col = (group_index * (group_size * HD)).astype(jnp.int32)
        kv_col = (group_index * HD).astype(jnp.int32)
        query_part = lax.dynamic_slice(held_queries, (first_row, query_col), (query_block, group_size * HD))
        query_part = query_part.astype(jnp.float32).reshape(query_block, group_size, HD)
        key_part = lax.dynamic_slice(held_keys, (zero_index, kv_col), (TOKENS, HD)).astype(jnp.float32)
        value_part = lax.dynamic_slice(held_values, (zero_index, kv_col), (TOKENS, HD)).astype(jnp.float32)
        query_pos = lax.dynamic_slice_in_dim(held_pos, first_row, query_block)
        query_doc = lax.dynamic_slice_in_dim(held_doc, first_row, query_block)
        query_lo = lax.dynamic_slice_in_dim(held_lo, first_row, query_block)
        allowed = (query_doc[:, None] == held_doc[None, :]) & (held_pos[None, :] <= query_pos[:, None]) & (key_block[None, :] >= query_lo[:, None])
        scores = jnp.einsum("tgd,sd->tgs", query_part, key_part) * score_scale
        scores = jnp.where(allowed[:, None, :], scores, -jnp.inf)
        row_max = jnp.max(scores, axis=-1, keepdims=True)
        weights = jnp.where(allowed[:, None, :], jnp.exp(scores - row_max), 0.0)
        denominators = jnp.sum(weights, axis=-1)
        rounded = lax.optimization_barrier(weights.astype(jnp.bfloat16)).astype(jnp.float32)
        result = jnp.einsum("tgs,sd->tgd", rounded, value_part) / denominators[..., None]
        return result.astype(jnp.bfloat16)

    results = lax.map(one_item, jnp.arange(KVH * block_total, dtype=jnp.int32))
    results = results.reshape(KVH, block_total, query_block, group_size, HD)
    held_att = results.transpose(1, 2, 0, 3, 4).reshape(TOKENS, query_width)
    held_blocks = held_att.reshape(NBLK, BLK, query_width)
    attended = jnp.zeros_like(held_blocks).at[inverse].set(held_blocks).reshape(TOKENS, query_width)
    feature_group = query_width // N_HEAD
    summed = jnp.zeros((TOKENS, D), jnp.float32)
    for group_part in range(N_HEAD):
        lower = group_part * feature_group
        partial_value = jnp.dot(attended[:, lower:lower + feature_group], out_weight[lower:lower + feature_group], preferred_element_type=jnp.float32)
        partial_value = lax.optimization_barrier(partial_value.astype(jnp.bfloat16)).astype(jnp.float32)
        summed = summed + partial_value
    return summed.astype(jnp.bfloat16)
```

```python
import functools

import jax
import jax.numpy as jnp
from jax import lax
from jax.experimental import pallas as pl
from jax.experimental.pallas import tpu as pltpu
from jax.sharding import PartitionSpec as P

HD = 128
BLK = 8
NEG = -1e30
EXP2_SCALE = HD**-0.5 * 1.4426950408889634
FAR = -(1 << 20)
SAFE = 104.0
UNROLL = 8
MIB = 1 << 20
VMEM = pltpu.VMEM


def shift(array, count, partner):
    pairs = [(i, partner(i)) for i in range(count)]
    return lax.ppermute(array, "ctx", [(i, j) for i, j in pairs if j is not None and 0 <= j < count])


def whole_vmem():
    return pl.BlockSpec(memory_space=VMEM)


def pack_body(ids, *refs):
    rows, width = refs[0].shape
    for out, keys, vals in ((refs[4], refs[0], refs[1]), (refs[5], refs[2], refs[3])):
        for r in range(0, rows, HD):
            for c in range(0, width, HD):
                out[r : r + HD, c : c + HD] = keys[r : r + HD, c : c + HD].T
        out[:, width:] = vals[...]


def pack(ids, key_rows, values, split):
    rows, width = key_rows.shape[0], key_rows.shape[1] // split
    kept = pl.BlockSpec((rows, width), lambda i, s: (0, s[0] % 2 if split == 2 else 0))
    sent = pl.BlockSpec((rows, width), lambda i, s: (0, 1 - s[0] % 2 if split == 2 else 0))
    out = jax.ShapeDtypeStruct((rows, 2 * width), key_rows.dtype)
    return pl.pallas_call(
        pack_body,
        out_shape=[out, out],
        grid_spec=pltpu.PrefetchScalarGridSpec(
            num_scalar_prefetch=1,
            grid=(1,),
            in_specs=[kept, kept, sent, sent],
            out_specs=[pl.BlockSpec(out.shape, lambda i, s: (0, 0))] * 2,
        ),
        compiler_params=pltpu.CompilerParams(vmem_limit_bytes=56 * MIB),
        name="pack",
    )(ids, key_rows, values, key_rows, values)


def other_half_body(ids, x_ref, o_ref):
    o_ref[...] = x_ref[...]


def other_half(ids, queries, parts=4):
    rows, half = queries.shape[0], queries.shape[1] // 2
    block = (rows, half // parts)
    return pl.pallas_call(
        other_half_body,
        out_shape=jax.ShapeDtypeStruct((rows, half), queries.dtype),
        grid_spec=pltpu.PrefetchScalarGridSpec(
            num_scalar_prefetch=1,
            grid=(parts,),
            in_specs=[pl.BlockSpec(block, lambda i, s: (0, (1 - s[0] % 2) * parts + i))],
            out_specs=pl.BlockSpec(block, lambda i, s: (0, i)),
        ),
        compiler_params=pltpu.CompilerParams(vmem_limit_bytes=56 * MIB),
        name="other_half",
    )(ids, queries)


def join_body(ids, mine, other, own, upper):
    rows = mine.shape[0]
    core = ids[0] % 2
    own[pl.ds(pl.multiple_of(core * rows, rows), rows), :] = mine[...]
    own[pl.ds(pl.multiple_of((1 - core) * rows, rows), rows), :] = other[...]
    upper[...] = own[rows:, :]


def join(ids, mine, other):
    rows, width = mine.shape
    return pl.pallas_call(
        join_body,
        out_shape=[
            jax.ShapeDtypeStruct((2 * rows, width), mine.dtype),
            jax.ShapeDtypeStruct((rows, width), mine.dtype),
        ],
        grid_spec=pltpu.PrefetchScalarGridSpec(
            num_scalar_prefetch=1,
            grid=(1,),
            in_specs=[pl.BlockSpec((rows, width), lambda i, s: (0, 0))] * 2,
            out_specs=[
                pl.BlockSpec((2 * rows, width), lambda i, s: (0, 0)),
                pl.BlockSpec((rows, width), lambda i, s: (0, 0)),
            ],
        ),
        compiler_params=pltpu.CompilerParams(vmem_limit_bytes=56 * MIB),
        name="join",
    )(ids, mine, other)


def attend_body(*refs, spans, arrays, group, heads, which, first, fetch, carried, final):
    ids, lows, highs = refs[:3]
    q_own, q_got, start_ref = refs[3:6]
    refs = refs[6:]
    keys, vals, refs = refs[:arrays], refs[arrays : 2 * arrays], refs[2 * arrays + carried :]
    if fetch:
        weight, refs = refs[0], refs[1:]
    acc, top, reach = refs[:3]
    refs = refs[max(carried, 3) :]
    if fetch:
        held_weight, refs = refs[0], refs[1:]
    if final:
        out_ref, refs = refs[0], refs[1:]
    q = refs[0]

    here = ids[0]
    core, column = here % 2, here // 2 % 2
    rows = q_own.shape[0]
    h = pl.program_id(0)
    t = {"both": lambda: pl.program_id(1), "own": lambda: core, "other": lambda: 1 - core}[which]()
    chip_base = (here - core) * rows
    row_base = chip_base + t * rows
    least, greatest = lows[t], highs[t]

    if fetch:
        columns = held_weight.shape[1]
        first_column = pl.multiple_of(ids[2] * columns, 128)
        copy = pltpu.make_async_copy(weight.at[:, pl.ds(first_column, columns)], held_weight, refs[1])
        pl.when((h == 0) & (pl.program_id(1) == 0))(copy.start)

    bases = [base(chip_base, column, rows) for _, _, _, base in spans]
    runs = [(b + s[2] > least) & (b < row_base + rows) for b, s in zip(bases, spans)]
    fulls = [(b >= greatest) & (b + s[2] <= row_base + 1) for b, s in zip(bases, spans)]

    @pl.when(functools.reduce(jnp.logical_or, runs))
    def _():
        @pl.when(t == core)
        def _():
            for g in range(group):
                q[g] = q_own[:, g * HD : (g + 1) * HD]

        @pl.when(t != core)
        def _():
            for g in range(group):
                q[g] = q_got[:, g * HD : (g + 1) * HD]

    def turned(i):
        array, at, width, _ = spans[i]
        return jnp.concatenate([keys[array][r : r + HD, :] for r in range(at, at + width, HD)], axis=1)

    def with_ones(i):
        array, at, width, _ = spans[i]
        v = vals[array][at : at + width, :]
        return jnp.concatenate([v, jnp.ones((width, HD), v.dtype)], axis=1)

    def bias_of(base, width):
        key_pos = base + lax.broadcasted_iota(jnp.int32, (rows, width), 1)
        row_pos = row_base + lax.broadcasted_iota(jnp.int32, (rows, width), 0)
        return jnp.where((key_pos <= row_pos) & (key_pos >= start_ref[0]), 0.0, NEG)

    def row_top(s):
        lane_top = s[:, :HD]
        for i in range(1, s.shape[1] // HD):
            lane_top = jnp.maximum(lane_top, s[:, i * HD : (i + 1) * HD])
        return jnp.max(lane_top, axis=1, keepdims=True)

    def weights_of(s, shift):
        wide = jnp.concatenate([shift] * (s.shape[1] // HD), axis=1)
        return jnp.exp2((s - wide) * EXP2_SCALE).astype(jnp.bfloat16)

    def step(chosen, masked, mode):
        kt = jnp.concatenate([turned(i) for i in chosen], axis=1)
        ve = jnp.concatenate([with_ones(i) for i in chosen], axis=0)
        if masked:
            bias = bias_of(bases[chosen[0]], kt.shape[1])

        def one_head(g, carry):
            q_here = q[g]
            s = jnp.dot(q_here, kt, preferred_element_type=jnp.float32)
            if masked:
                s = s + bias
            if mode == "first":
                m = jnp.broadcast_to(row_top(s), (rows, HD))
                top[h, t, g] = m
                acc[h, t, g] = jnp.dot(weights_of(s, m), ve, preferred_element_type=jnp.float32)
                sizes = jnp.abs(q_here.astype(jnp.float32))
                longest = jnp.maximum(carry[0], jnp.max(sizes.reshape(rows // 8, 8, HD), axis=0))
                lowest = jnp.minimum(carry[1], jnp.min(m.reshape(rows // 8, 8, HD), axis=0))
                return longest, lowest
            if mode == "kept":
                acc[h, t, g] += jnp.dot(weights_of(s, top[h, t, g]), ve, preferred_element_type=jnp.float32)
            else:
                m_old = top[h, t, g]
                m = jnp.maximum(m_old, row_top(s))
                fade = jnp.exp2((m_old - m) * EXP2_SCALE)
                update = jnp.dot(weights_of(s, m), ve, preferred_element_type=jnp.float32)
                top[h, t, g] = m
                acc[h, t, g] = acc[h, t, g] * jnp.concatenate([fade, fade], axis=1) + update
            return carry

        def some_heads(at, carry):
            for i in range(UNROLL):
                carry = one_head(at * UNROLL + i, carry)
            return carry

        carry = (jnp.zeros((8, HD), jnp.float32), jnp.full((8, HD), -NEG)) if mode == "first" else 0
        carry = lax.fori_loop(0, group // UNROLL, some_heads, carry)
        if mode == "first":
            reach[h, t, 0], reach[h, t, 1] = carry

    everything = list(range(len(spans)))
    if first:
        pl.when(t == 0)(lambda: step([0], True, "first"))
        pl.when(t == 1)(lambda: step(everything, True, "first"))
    else:
        room = jnp.min(reach[h, t, 1]) + SAFE / EXP2_SCALE
        widest = jnp.max(reach[h, t, 0], axis=0, keepdims=True)
        kt = jnp.concatenate([turned(i) for i in everything], axis=1).astype(jnp.float32)
        norms = jnp.max(jnp.sum(kt * kt, axis=0, keepdims=True), axis=1, keepdims=True)
        most = jnp.max(norms * jnp.sum(widest * widest, axis=1, keepdims=True)) * 1.01
        safe = (room > 0.0) & (most <= room * room)
        together = functools.reduce(jnp.logical_and, fulls) & safe
        pl.when(together)(lambda: step(everything, False, "kept"))
        for i in everything:
            alone = runs[i] & jnp.logical_not(together)
            pl.when(alone & safe)(functools.partial(step, [i], True, "kept"))
            pl.when(alone & jnp.logical_not(safe))(functools.partial(step, [i], True, "moved"))

    if fetch:
        pl.when((h == heads - 1) & (pl.program_id(1) == pl.num_programs(1) - 1))(copy.wait)
    if final:
        for g in range(group):
            a = acc[h, t, g]
            out_ref[:, g * HD : (g + 1) * HD] = (a[:, :HD] / a[:, HD:]).astype(jnp.bfloat16)


def attend(scalars, queries, got_queries, starts, pieces, spans, state, group, heads, which, weight=None, columns=0):
    rows, width = queries.shape[0], group * HD
    first, fetch, final = state is None, weight is not None, which != "both"
    tiles = 2 if which == "both" else 1

    def tile_of(t, ids):
        return {"both": t, "own": ids[0] % 2, "other": 1 - ids[0] % 2}[which]

    in_specs = [
        pl.BlockSpec((rows, width), lambda h, t, i, *_: (0, i[0] % 2 * heads + h)),
        pl.BlockSpec((rows, width), lambda h, t, *_: (0, h)),
        pl.BlockSpec((1, rows, 1), lambda h, t, i, *_: (tile_of(t, i), 0, 0)),
    ]
    in_specs += [pl.BlockSpec((p.shape[0], HD), lambda h, t, *_: (0, h)) for p in pieces]
    in_specs += [pl.BlockSpec((p.shape[0], HD), lambda h, t, *_: (0, heads + h)) for p in pieces]
    operands = [*scalars, queries, got_queries, starts, *pieces, *pieces]
    out_shape = [
        VMEM((heads, 2, group, rows, 2 * HD), jnp.float32),
        VMEM((heads, 2, group, rows, HD), jnp.float32),
        VMEM((heads, 2, 2, 8, HD), jnp.float32),
    ]
    aliases = {}
    if not first:
        out_shape = [VMEM(a.shape, a.dtype) for a in state]
        aliases = {len(operands) + i: i for i in range(len(state))}
        operands += state
        in_specs += [whole_vmem()] * len(state)
    out_specs = [whole_vmem()] * len(out_shape)
    scratch = [VMEM((group, rows, HD), queries.dtype)]
    if fetch:
        operands.append(weight)
        in_specs.append(pl.BlockSpec(memory_space=pl.ANY))
        out_shape.append(VMEM((weight.shape[0], columns), weight.dtype))
        out_specs.append(whole_vmem())
        scratch.append(pltpu.SemaphoreType.DMA)
    if final:
        out_shape.append(jax.ShapeDtypeStruct((rows, heads * width), queries.dtype))
        out_specs.append(pl.BlockSpec((rows, width), lambda h, t, *_: (0, h)))
    keys = sum(s[2] for s in spans)
    pairs = heads * tiles * rows * group * keys
    return pl.pallas_call(
        functools.partial(
            attend_body,
            spans=spans,
            arrays=len(pieces),
            group=group,
            heads=heads,
            which=which,
            first=first,
            fetch=fetch,
            carried=0 if first else len(state),
            final=final,
        ),
        out_shape=out_shape,
        grid_spec=pltpu.PrefetchScalarGridSpec(
            num_scalar_prefetch=3,
            grid=(heads, tiles),
            in_specs=in_specs,
            out_specs=out_specs,
            scratch_shapes=scratch,
        ),
        input_output_aliases=aliases,
        compiler_params=pltpu.CompilerParams(vmem_limit_bytes=14 * MIB),
        cost_estimate=pl.CostEstimate(flops=8 * pairs * HD, bytes_accessed=4 * MIB, transcendentals=pairs),
        name=f"attend_{which}_{keys}",
    )(*operands)


def project_held_body(ids, a_ref, b_ref, w_ref, alias, o_ref, *, at, tile):
    half = a_ref.shape[1]
    core = ids[0] % 2
    mine = pl.ds(pl.multiple_of(core * half, half), half)
    theirs = pl.ds(pl.multiple_of((1 - core) * half, half), half)
    for n in range(o_ref.shape[1] // tile):
        cols = slice(at + n * tile, at + (n + 1) * tile)
        total = jnp.dot(a_ref[...], w_ref[mine, cols], preferred_element_type=jnp.float32)
        total = total + jnp.dot(b_ref[...], w_ref[theirs, cols], preferred_element_type=jnp.float32)
        o_ref[:, n * tile : (n + 1) * tile] = total.astype(o_ref.dtype)


def project_held(ids, a, b, held, at, columns):
    rows, half = a.shape
    block = lambda shape: pl.BlockSpec(shape, lambda i, s: (0, 0))
    return pl.pallas_call(
        functools.partial(project_held_body, at=at, tile=min(256, columns)),
        out_shape=[VMEM(held.shape, held.dtype), jax.ShapeDtypeStruct((rows, columns), a.dtype)],
        grid_spec=pltpu.PrefetchScalarGridSpec(
            num_scalar_prefetch=1,
            grid=(1,),
            in_specs=[block((rows, half)), block((rows, half)), whole_vmem()],
            out_specs=[whole_vmem(), block((rows, columns))],
        ),
        input_output_aliases={3: 0},
        compiler_params=pltpu.CompilerParams(vmem_limit_bytes=16 * MIB),
        cost_estimate=pl.CostEstimate(flops=4 * rows * half * columns, bytes_accessed=2 * MIB, transcendentals=0),
        name="project_held",
    )(ids, a, b, held)


def project_body(ids, a_ref, b_ref, wa_ref, wb_ref, o_ref):
    total = jnp.dot(a_ref[...], wa_ref[...], preferred_element_type=jnp.float32)
    total = total + jnp.dot(b_ref[...], wb_ref[...], preferred_element_type=jnp.float32)
    o_ref[...] = total.astype(o_ref.dtype)


def project(ids, a, b, weight, columns, tile):
    rows, half = a.shape
    tiles = columns // tile
    block = pl.BlockSpec((rows, half), lambda n, s: (0, 0))
    return pl.pallas_call(
        project_body,
        out_shape=jax.ShapeDtypeStruct((rows, columns), a.dtype),
        grid_spec=pltpu.PrefetchScalarGridSpec(
            num_scalar_prefetch=1,
            grid=(tiles,),
            in_specs=[
                block,
                block,
                pl.BlockSpec((half, tile), lambda n, s: (s[0] % 2, s[1] * tiles + n)),
                pl.BlockSpec((half, tile), lambda n, s: (1 - s[0] % 2, s[1] * tiles + n)),
            ],
            out_specs=pl.BlockSpec((rows, tile), lambda n, s: (0, n)),
        ),
        compiler_params=pltpu.CompilerParams(vmem_limit_bytes=48 * MIB),
        cost_estimate=pl.CostEstimate(
            flops=4 * rows * half * columns, bytes_accessed=4 * half * columns, transcendentals=0
        ),
        name="project",
    )(ids, a, b, weight, weight)


def on_device(queries, key_rows, values, lengths, block_plan, inverse, mask_lo, out_weight):
    rows, query_width = queries.shape
    kv_heads = key_rows.shape[1] // HD
    count, head_count = lax.axis_size("ctx"), lax.axis_size("head")
    here, head_here = lax.axis_index("ctx"), lax.axis_index("head")
    core = here % 2
    split = 2 if kv_heads % 2 == 0 else 1
    heads = kv_heads // split
    half = query_width // 2
    group = half // (heads * HD)
    levels = count // 8

    place = jnp.arange(3, dtype=jnp.int32)
    send_half = 1 - head_here if head_count == 2 else 0
    ids = jnp.where(place == 0, here, jnp.where(place == 1, head_here, send_half)).astype(jnp.int32)

    sibling = functools.partial(shift, count=count, partner=lambda i: i ^ 1)
    mine, send = pack(ids, key_rows, values, split)
    swapped = sibling(send)
    queries_late, _ = lax.optimization_barrier((queries, send))
    sent_queries = other_half(ids, queries_late)
    swapped, _ = lax.optimization_barrier((swapped, sent_queries))
    own, upper = join(ids, mine, swapped)
    sent_queries, _ = lax.optimization_barrier((sent_queries, own))
    got_queries = sibling(sent_queries)

    chip_base = (here - core) * rows
    doc_ends = jnp.cumsum(lengths)
    pos = chip_base + jnp.arange(2 * rows, dtype=jnp.int32)
    doc_start = jnp.max(jnp.where(doc_ends[None, :] <= pos[:, None], doc_ends[None, :], 0), axis=1)
    low = lax.dynamic_slice_in_dim(mask_lo, chip_base // BLK, 2 * rows // BLK) * BLK
    starts = jnp.maximum(doc_start, jnp.repeat(low, BLK)).astype(jnp.int32).reshape(2, rows)
    scalars = (ids, jnp.min(starts, axis=1), jnp.max(starts, axis=1))
    start_columns = starts[:, :, None]

    common = (scalars, queries, got_queries, start_columns)
    near = shift(own, count, lambda i: i + 2 if i // 2 % 2 == 0 else None)
    moving = shift(own, count, lambda i: i + 4)
    own_spans = [(0, 0, rows, lambda base, column, r: base), (0, rows, rows, lambda base, column, r: base + r)]
    state = attend(*common, [own], own_spans, None, group, heads, "both")
    keep = out_weight.shape[1] // head_count
    held_columns = keep if head_count == 2 else out_weight.shape[1]

    before, at_before = near, lambda base, column, r: jnp.where(column == 1, base - 2 * r, FAR)
    for d in range(1, levels + 1):
        moving, _ = lax.optimization_barrier((moving, state[2]))
        crossed = shift(moving, count, lambda i: i ^ 2)
        at_level = lambda base, column, r, d=d: base - 4 * d * r
        at_cross = lambda base, column, r, d=d: base - 4 * d * r + jnp.where(column == 0, 2 * r, -2 * r)
        onward = shift(moving, count, lambda i: i + 4) if d < levels else None
        if d == 1:
            reach = 4 * (levels + 1) - 2
            upper, _ = lax.optimization_barrier((upper, moving))
            last = shift(upper, count, lambda i: i + reach if i // 2 % 2 == 1 else None)
        spans = [(0, 0, 2 * rows, at_before), (1, 0, 2 * rows, at_level)]
        fetch = (out_weight, held_columns) if d == levels else ()
        state = attend(*common, [before, moving], spans, state, group, heads, "both", *fetch)
        before, at_before, moving = crossed, at_cross, onward
    at_last = lambda base, column, r: jnp.where(column == 0, base - reach * r + r, FAR)
    spans = [
        (0, 0, rows, at_before),
        (0, rows, rows, lambda base, column, r: at_before(base, column, r) + r),
        (1, 0, rows, at_last),
    ]
    *state, theirs = attend(*common, [before, last], spans, state, group, heads, "other")
    got = sibling(theirs)
    *state, att = attend(*common, [before, last], spans, state, group, heads, "own")
    held = state[3]

    if head_count != 2:
        _, partial_sums = project_held(ids, att, got, held, 0, held_columns)
        return lax.psum_scatter(partial_sums, "head", scatter_dimension=1, tiled=True)
    arrived = []
    chunks = 2
    for c in range(chunks):
        held, sent = project_held(ids, att, got, held, c * keep // chunks, keep // chunks)
        arrived.append(lax.ppermute(sent, "head", [(0, 1), (1, 0)]))
    kept = project(ids, att, got, out_weight, keep, 256)
    return (kept.astype(jnp.float32) + jnp.concatenate(arrived, axis=1).astype(jnp.float32)).astype(jnp.bfloat16)


def solution(mesh):
    in_specs = (
        P("ctx", "head"),
        P("ctx", "head"),
        P("ctx", "head"),
        P(),
        P("ctx"),
        P(),
        P(),
        P("head", None),
    )
    return jax.shard_map(
        on_device, mesh=mesh, in_specs=in_specs, out_specs=P("ctx", "head"), check_vma=False
    )
```

```python
import functools

import jax
import jax.numpy as jnp
from jax import lax
from jax.experimental import pallas as pl
from jax.experimental.pallas import tpu as pltpu
from jax.sharding import PartitionSpec as P

HD = 128
BLK = 8
NEG = -1e30
EXP2_SCALE = HD**-0.5 * 1.4426950408889634
FAR = -(1 << 20)
SAFE = 104.0
MIB = 1 << 20
VMEM = pltpu.VMEM
SMALL = pl.CostEstimate(flops=1 << 20, bytes_accessed=1 << 16, transcendentals=0)


def shift(array, count, partner):
    pairs = [(i, partner(i)) for i in range(count)]
    return lax.ppermute(array, "ctx", [(i, j) for i, j in pairs if j is not None and 0 <= j < count])


def whole_vmem():
    return pl.BlockSpec(memory_space=VMEM)


def pack_body(ids, key_rows, values, queries, mine, send, sent_queries, keys, vals, sems, *, split):
    core = ids[0] % 2
    rows, width = keys.shape
    half = sent_queries.shape[1]
    theirs = pl.ds(pl.multiple_of((1 - core) * half, half), half)
    copies = [
        pltpu.make_async_copy(key_rows, keys, sems.at[0]),
        pltpu.make_async_copy(values, vals, sems.at[1]),
        pltpu.make_async_copy(queries.at[:, theirs], sent_queries, sems.at[2]),
    ]
    for copy in copies:
        copy.start()
    part = width // split
    copies[0].wait()
    for out, side in ((send, 1 - core), (mine, core)):
        first = pl.multiple_of(side * part if split == 2 else 0, HD)
        for r in range(0, rows, HD):
            for c in range(0, part, HD):
                out[r : r + HD, c : c + HD] = keys[r : r + HD, pl.ds(first + c, HD)].T
    copies[1].wait()
    for out, side in ((send, 1 - core), (mine, core)):
        first = pl.multiple_of(side * part if split == 2 else 0, HD)
        out[:, part:] = vals[:, pl.ds(first, part)]
    copies[2].wait()


def in_hbm(array):
    return pltpu.with_memory_space_constraint(array, pltpu.HBM)


def pack(ids, key_rows, values, queries, split):
    rows, width = key_rows.shape
    out = VMEM((rows, 2 * (width // split)), key_rows.dtype)
    return pl.pallas_call(
        functools.partial(pack_body, split=split),
        out_shape=[out, out, jax.ShapeDtypeStruct((rows, queries.shape[1] // 2), queries.dtype)],
        grid_spec=pltpu.PrefetchScalarGridSpec(
            num_scalar_prefetch=1,
            grid=(1,),
            in_specs=[pl.BlockSpec(memory_space=pl.ANY)] * 3,
            out_specs=[whole_vmem(), whole_vmem(), pl.BlockSpec(memory_space=pl.ANY)],
            scratch_shapes=[
                VMEM((rows, width), key_rows.dtype),
                VMEM((rows, width), key_rows.dtype),
                pltpu.SemaphoreType.DMA((3,)),
            ],
        ),
        compiler_params=pltpu.CompilerParams(vmem_limit_bytes=8 * MIB),
        name="pack",
    )(ids, in_hbm(key_rows), in_hbm(values), in_hbm(queries))


def join_body(ids, mine, other, own, upper):
    rows = mine.shape[0]
    core = ids[0] % 2
    own[pl.ds(pl.multiple_of(core * rows, rows), rows), :] = mine[...]
    own[pl.ds(pl.multiple_of((1 - core) * rows, rows), rows), :] = other[...]
    upper[...] = own[rows:, :]


def join(ids, mine, other):
    rows, width = mine.shape
    return pl.pallas_call(
        join_body,
        out_shape=[
            jax.ShapeDtypeStruct((2 * rows, width), mine.dtype),
            jax.ShapeDtypeStruct((rows, width), mine.dtype),
        ],
        grid_spec=pltpu.PrefetchScalarGridSpec(
            num_scalar_prefetch=1,
            grid=(1,),
            in_specs=[pl.BlockSpec((rows, width), lambda i, s: (0, 0))] * 2,
            out_specs=[
                pl.BlockSpec((2 * rows, width), lambda i, s: (0, 0)),
                pl.BlockSpec((rows, width), lambda i, s: (0, 0)),
            ],
        ),
        compiler_params=pltpu.CompilerParams(vmem_limit_bytes=8 * MIB),
        name="join",
    )(ids, mine, other)


def attend_body(*refs, spans, arrays, group, heads, which, first, fetch, carried, final):
    ids, lows, highs = refs[:3]
    q_own, q_got, start_ref = refs[3:6]
    refs = refs[6:]
    keys, vals, refs = refs[:arrays], refs[arrays : 2 * arrays], refs[2 * arrays + carried :]
    if fetch:
        weight, refs = refs[0], refs[1:]
    acc, top, reach = refs[:3]
    refs = refs[max(carried, 3) :]
    if fetch:
        held_weight, refs = refs[0], refs[1:]
    if final:
        out_ref, refs = refs[0], refs[1:]
    q, some_keys, some_values = refs[:3]

    here = ids[0]
    core, column = here % 2, here // 2 % 2
    rows = q_own.shape[0]
    h = pl.program_id(0)
    t = {"both": lambda: pl.program_id(1), "own": lambda: core, "other": lambda: 1 - core}[which]()
    chip_base = (here - core) * rows
    row_base = chip_base + t * rows
    least, greatest = lows[t], highs[t]

    if fetch:
        columns = held_weight.shape[1]
        first_column = pl.multiple_of(ids[2] * columns, 128)
        copy = pltpu.make_async_copy(weight.at[:, pl.ds(first_column, columns)], held_weight, refs[3])
        pl.when((h == 0) & (pl.program_id(1) == 0))(copy.start)

    bases = [base(chip_base, column, rows) for _, _, _, base in spans]
    runs = [(b + s[2] > least) & (b < row_base + rows) for b, s in zip(bases, spans)]
    fulls = [(b >= greatest) & (b + s[2] <= row_base + 1) for b, s in zip(bases, spans)]

    @pl.when(functools.reduce(jnp.logical_or, runs))
    def _():
        @pl.when(t == core)
        def _():
            for g in range(group):
                q[g] = q_own[:, g * HD : (g + 1) * HD]

        @pl.when(t != core)
        def _():
            for g in range(group):
                q[g] = q_got[:, g * HD : (g + 1) * HD]

    def turned(i):
        array, at, width, _ = spans[i]
        return jnp.concatenate([keys[array][r : r + HD, :] for r in range(at, at + width, HD)], axis=1)

    def with_ones(i):
        array, at, width, _ = spans[i]
        v = vals[array][at : at + width, :]
        return jnp.concatenate([v, jnp.ones((width, HD), v.dtype)], axis=1)

    def bias_of(base, width):
        key_pos = base + lax.broadcasted_iota(jnp.int32, (rows, width), 1)
        row_pos = row_base + lax.broadcasted_iota(jnp.int32, (rows, width), 0)
        starts = jnp.broadcast_to(start_ref[0].astype(jnp.float32), (HD, rows)).T
        starts = jnp.concatenate([starts] * (width // HD), axis=1)
        return jnp.where((key_pos <= row_pos) & (key_pos.astype(jnp.float32) >= starts), 0.0, NEG)

    def row_top(s):
        lane_top = s[:, :HD]
        for i in range(1, s.shape[1] // HD):
            lane_top = jnp.maximum(lane_top, s[:, i * HD : (i + 1) * HD])
        return jnp.max(lane_top, axis=1, keepdims=True)

    def weights_of(s, shift):
        wide = jnp.concatenate([shift] * (s.shape[1] // HD), axis=1)
        return jnp.exp2((s - wide) * EXP2_SCALE).astype(jnp.bfloat16)

    def step(kt, ve, base, mode, unroll):
        masked = base is not None
        if masked:
            bias = bias_of(base, kt.shape[1])

        def one_head(g, carry):
            q_here = q[g]
            s = jnp.dot(q_here, kt, preferred_element_type=jnp.float32)
            if masked:
                s = s + bias
            if mode == "first":
                m = jnp.broadcast_to(row_top(s), (rows, HD))
                top[h, t, g] = m
                acc[h, t, g] = jnp.dot(weights_of(s, m), ve, preferred_element_type=jnp.float32)
                sizes = jnp.abs(q_here.astype(jnp.float32))
                longest = jnp.maximum(carry[0], jnp.max(sizes.reshape(rows // 8, 8, HD), axis=0))
                lowest = jnp.minimum(carry[1], jnp.min(m.reshape(rows // 8, 8, HD), axis=0))
                return longest, lowest
            if mode == "kept":
                acc[h, t, g] += jnp.dot(weights_of(s, top[h, t, g]), ve, preferred_element_type=jnp.float32)
            else:
                m_old = top[h, t, g]
                m = jnp.maximum(m_old, row_top(s))
                fade = jnp.exp2((m_old - m) * EXP2_SCALE)
                update = jnp.dot(weights_of(s, m), ve, preferred_element_type=jnp.float32)
                top[h, t, g] = m
                acc[h, t, g] = acc[h, t, g] * jnp.concatenate([fade, fade], axis=1) + update
            return carry

        def some_heads(at, carry):
            for i in range(unroll):
                carry = one_head(at * unroll + i, carry)
            return carry

        carry = (jnp.zeros((8, HD), jnp.float32), jnp.full((8, HD), -NEG)) if mode == "first" else 0
        carry = lax.fori_loop(0, group // unroll, some_heads, carry)
        if mode == "first":
            reach[h, t, 0], reach[h, t, 1] = carry

    def all_keys(count):
        return jnp.concatenate([turned(i) for i in range(count)], axis=1)

    def all_values(count):
        return jnp.concatenate([with_ones(i) for i in range(count)], axis=0)

    count = len(spans)
    if first:
        pl.when(t == 0)(lambda: step(all_keys(1), all_values(1), bases[0], "first", group))
        pl.when(t == 1)(lambda: step(all_keys(count), all_values(count), bases[0], "first", group))
    else:
        room = jnp.min(reach[h, t, 1]) + SAFE / EXP2_SCALE
        widest = jnp.max(reach[h, t, 0], axis=0, keepdims=True)
        kt = all_keys(count).astype(jnp.float32)
        norms = jnp.max(jnp.sum(kt * kt, axis=0, keepdims=True), axis=1, keepdims=True)
        most = jnp.max(norms * jnp.sum(widest * widest, axis=1, keepdims=True)) * 1.01
        safe = (room > 0.0) & (most <= room * room)
        together = functools.reduce(jnp.logical_and, fulls) & safe
        pl.when(together)(lambda: step(all_keys(count), all_values(count), None, "kept", group))

        def one_piece(piece, carry):
            choose = lambda options: functools.reduce(
                lambda rest, i: jnp.where(piece == i, options[i], rest), range(1, count), options[0]
            )
            base = choose(bases)
            run = choose([jnp.int32(r) for r in runs]) == 1

            @pl.when(run)
            def _():
                for i in range(count):

                    @pl.when(piece == i)
                    def _(i=i):
                        some_keys[...] = turned(i)
                        some_values[...] = with_ones(i)

            pl.when(run & safe)(lambda: step(some_keys[...], some_values[...], base, "kept", group))
            pl.when(run & jnp.logical_not(safe))(lambda: step(some_keys[...], some_values[...], base, "moved", 1))
            return carry

        @pl.when(jnp.logical_not(together))
        def _():
            lax.fori_loop(0, count, one_piece, 0)

    if fetch:
        pl.when((h == heads - 1) & (pl.program_id(1) == pl.num_programs(1) - 1))(copy.wait)
    if final:
        for g in range(group):
            a = acc[h, t, g]
            out_ref[:, g * HD : (g + 1) * HD] = (a[:, :HD] / a[:, HD:]).astype(jnp.bfloat16)


def attend(scalars, queries, got_queries, starts, pieces, spans, state, group, heads, which, weight=None, columns=0):
    rows, width = queries.shape[0], group * HD
    first, fetch, final = state is None, weight is not None, which != "both"
    tiles = 2 if which == "both" else 1

    def tile_of(t, ids):
        return {"both": t, "own": ids[0] % 2, "other": 1 - ids[0] % 2}[which]

    in_specs = [
        pl.BlockSpec((rows, width), lambda h, t, i, *_: (0, i[0] % 2 * heads + h)),
        pl.BlockSpec((rows, width), lambda h, t, *_: (0, h)),
        pl.BlockSpec((1, 1, rows), lambda h, t, i, *_: (tile_of(t, i), 0, 0)),
    ]
    in_specs += [pl.BlockSpec((p.shape[0], HD), lambda h, t, *_: (0, h)) for p in pieces]
    in_specs += [pl.BlockSpec((p.shape[0], HD), lambda h, t, *_: (0, heads + h)) for p in pieces]
    operands = [*scalars, in_hbm(queries), in_hbm(got_queries), starts, *pieces, *pieces]
    out_shape = [
        VMEM((heads, 2, group, rows, 2 * HD), jnp.float32),
        VMEM((heads, 2, group, rows, HD), jnp.float32),
        VMEM((heads, 2, 2, 8, HD), jnp.float32),
    ]
    aliases = {}
    if not first:
        out_shape = [VMEM(a.shape, a.dtype) for a in state]
        aliases = {len(operands) + i: i for i in range(len(state))}
        operands += state
        in_specs += [whole_vmem()] * len(state)
    out_specs = [whole_vmem()] * len(out_shape)
    wide = spans[0][2]
    scratch = [
        VMEM((group, rows, HD), queries.dtype),
        VMEM((HD, wide), queries.dtype),
        VMEM((wide, 2 * HD), queries.dtype),
    ]
    if fetch:
        operands.append(weight)
        in_specs.append(pl.BlockSpec(memory_space=pl.ANY))
        out_shape.append(VMEM((weight.shape[0], columns), weight.dtype))
        out_specs.append(whole_vmem())
        scratch.append(pltpu.SemaphoreType.DMA)
    if final:
        out_shape.append(jax.ShapeDtypeStruct((rows, heads * width), queries.dtype))
        out_specs.append(pl.BlockSpec((rows, width), lambda h, t, *_: (0, h)))
    keys = sum(s[2] for s in spans)
    return pl.pallas_call(
        functools.partial(
            attend_body,
            spans=spans,
            arrays=len(pieces),
            group=group,
            heads=heads,
            which=which,
            first=first,
            fetch=fetch,
            carried=0 if first else len(state),
            final=final,
        ),
        out_shape=out_shape,
        grid_spec=pltpu.PrefetchScalarGridSpec(
            num_scalar_prefetch=3,
            grid=(heads, tiles),
            in_specs=in_specs,
            out_specs=out_specs,
            scratch_shapes=scratch,
        ),
        input_output_aliases=aliases,
        compiler_params=pltpu.CompilerParams(vmem_limit_bytes=14 * MIB),
        cost_estimate=SMALL,
        name=f"attend_{which}_{keys}",
    )(*operands)


def project_held_body(ids, a_ref, b_ref, w_ref, alias, o_ref, *, at, tile):
    half = a_ref.shape[1]
    core = ids[0] % 2
    mine = pl.ds(pl.multiple_of(core * half, half), half)
    theirs = pl.ds(pl.multiple_of((1 - core) * half, half), half)
    for n in range(o_ref.shape[1] // tile):
        cols = slice(at + n * tile, at + (n + 1) * tile)
        total = jnp.dot(a_ref[...], w_ref[mine, cols], preferred_element_type=jnp.float32)
        total = total + jnp.dot(b_ref[...], w_ref[theirs, cols], preferred_element_type=jnp.float32)
        o_ref[:, n * tile : (n + 1) * tile] = total.astype(o_ref.dtype)


def project_held(ids, a, b, held, at, columns):
    rows, half = a.shape
    block = lambda shape: pl.BlockSpec(shape, lambda i, s: (0, 0))
    return pl.pallas_call(
        functools.partial(project_held_body, at=at, tile=min(256, columns)),
        out_shape=[VMEM(held.shape, held.dtype), jax.ShapeDtypeStruct((rows, columns), a.dtype)],
        grid_spec=pltpu.PrefetchScalarGridSpec(
            num_scalar_prefetch=1,
            grid=(1,),
            in_specs=[block((rows, half)), block((rows, half)), whole_vmem()],
            out_specs=[whole_vmem(), block((rows, columns))],
        ),
        input_output_aliases={3: 0},
        compiler_params=pltpu.CompilerParams(vmem_limit_bytes=16 * MIB),
        cost_estimate=pl.CostEstimate(flops=4 * rows * half * columns, bytes_accessed=2 * MIB, transcendentals=0),
        name="project_held",
    )(ids, a, b, held)


def project_body(ids, a_ref, b_ref, wa_ref, wb_ref, o_ref):
    total = jnp.dot(a_ref[...], wa_ref[...], preferred_element_type=jnp.float32)
    total = total + jnp.dot(b_ref[...], wb_ref[...], preferred_element_type=jnp.float32)
    o_ref[...] = total.astype(o_ref.dtype)


def project(ids, a, b, weight, columns, tile):
    rows, half = a.shape
    tiles = columns // tile
    block = pl.BlockSpec((rows, half), lambda n, s: (0, 0))
    return pl.pallas_call(
        project_body,
        out_shape=jax.ShapeDtypeStruct((rows, columns), a.dtype),
        grid_spec=pltpu.PrefetchScalarGridSpec(
            num_scalar_prefetch=1,
            grid=(tiles,),
            in_specs=[
                block,
                block,
                pl.BlockSpec((half, tile), lambda n, s: (s[0] % 2, s[1] * tiles + n)),
                pl.BlockSpec((half, tile), lambda n, s: (1 - s[0] % 2, s[1] * tiles + n)),
            ],
            out_specs=pl.BlockSpec((rows, tile), lambda n, s: (0, n)),
        ),
        compiler_params=pltpu.CompilerParams(vmem_limit_bytes=48 * MIB),
        cost_estimate=pl.CostEstimate(
            flops=4 * rows * half * columns, bytes_accessed=4 * half * columns, transcendentals=0
        ),
        name="project",
    )(ids, a, b, weight, weight)


def on_device(queries, key_rows, values, lengths, block_plan, inverse, mask_lo, out_weight):
    rows, query_width = queries.shape
    kv_heads = key_rows.shape[1] // HD
    count, head_count = lax.axis_size("ctx"), lax.axis_size("head")
    here, head_here = lax.axis_index("ctx"), lax.axis_index("head")
    core = here % 2
    split = 2 if kv_heads % 2 == 0 else 1
    heads = kv_heads // split
    half = query_width // 2
    group = half // (heads * HD)
    levels = count // 8

    place = jnp.arange(3, dtype=jnp.int32)
    send_half = 1 - head_here if head_count == 2 else 0
    ids = jnp.where(place == 0, here, jnp.where(place == 1, head_here, send_half)).astype(jnp.int32)

    sibling = functools.partial(shift, count=count, partner=lambda i: i ^ 1)
    mine, send, sent_queries = pack(ids, key_rows, values, queries, split)
    swapped = sibling(send)
    up_level = functools.partial(shift, count=count, partner=lambda i: i + 4)
    first_hop = [up_level(mine), up_level(swapped)]
    own, upper = join(ids, mine, swapped)
    sent_queries, lengths, mask_lo, _ = lax.optimization_barrier((sent_queries, lengths, mask_lo, swapped))
    got_queries = sibling(sent_queries)

    chip_base = (here - core) * rows
    doc_ends = jnp.cumsum(lengths)
    pos = chip_base + jnp.arange(2 * rows, dtype=jnp.int32)
    doc_start = jnp.max(jnp.where(doc_ends[None, :] <= pos[:, None], doc_ends[None, :], 0), axis=1)
    low = lax.dynamic_slice_in_dim(mask_lo, chip_base // BLK, 2 * rows // BLK) * BLK
    starts = jnp.maximum(doc_start, jnp.repeat(low, BLK)).astype(jnp.int32).reshape(2, rows)
    scalars = (ids, jnp.min(starts, axis=1), jnp.max(starts, axis=1))
    start_rows = starts[:, None, :]

    common = (scalars, queries, got_queries, start_rows)
    near = shift(own, count, lambda i: i + 2 if i // 2 % 2 == 0 else None)
    own_spans = [(0, 0, rows, lambda base, column, r: base), (0, rows, rows, lambda base, column, r: base + r)]
    state = attend(*common, [own], own_spans, None, group, heads, "both")
    keep = out_weight.shape[1] // head_count
    held_columns = keep if head_count == 2 else out_weight.shape[1]

    before, at_before = near, lambda base, column, r: jnp.where(column == 1, base - 2 * r, FAR)
    for d in range(1, levels + 1):
        if d == 1:
            first_hop = lax.optimization_barrier((*first_hop, state[2]))[:2]
            moving, _ = join(ids, *first_hop)
        else:
            moving, _ = lax.optimization_barrier((moving, state[2]))
        crossed = shift(moving, count, lambda i: i ^ 2)
        at_level = lambda base, column, r, d=d: base - 4 * d * r
        at_cross = lambda base, column, r, d=d: base - 4 * d * r + jnp.where(column == 0, 2 * r, -2 * r)
        onward = shift(moving, count, lambda i: i + 4) if d < levels else None
        if d == 1:
            reach = 4 * (levels + 1) - 2
            upper, _ = lax.optimization_barrier((upper, moving))
            last = shift(upper, count, lambda i: i + reach if i // 2 % 2 == 1 else None)
        spans = [(0, 0, 2 * rows, at_before), (1, 0, 2 * rows, at_level)]
        fetch = (out_weight, held_columns) if d == levels else ()
        state = attend(*common, [before, moving], spans, state, group, heads, "both", *fetch)
        before, at_before, moving = crossed, at_cross, onward
    at_last = lambda base, column, r: jnp.where(column == 0, base - reach * r + r, FAR)
    spans = [
        (0, 0, rows, at_before),
        (0, rows, rows, lambda base, column, r: at_before(base, column, r) + r),
        (1, 0, rows, at_last),
    ]
    *state, theirs = attend(*common, [before, last], spans, state, group, heads, "other")
    got = sibling(theirs)
    *state, att = attend(*common, [before, last], spans, state, group, heads, "own")
    held = state[3]

    if head_count != 2:
        _, partial_sums = project_held(ids, att, got, held, 0, held_columns)
        return lax.psum_scatter(partial_sums, "head", scatter_dimension=1, tiled=True)
    arrived = []
    for at, columns in ((0, keep // 2), (keep // 2, keep // 2)):
        held, sent = project_held(ids, att, got, held, at, columns)
        arrived.append(lax.ppermute(sent, "head", [(0, 1), (1, 0)]))
    kept = project(ids, att, got, out_weight, keep, 256)
    return (kept.astype(jnp.float32) + jnp.concatenate(arrived, axis=1).astype(jnp.float32)).astype(jnp.bfloat16)


def solution(mesh):
    in_specs = (
        P("ctx", "head"),
        P("ctx", "head"),
        P("ctx", "head"),
        P(),
        P("ctx"),
        P(),
        P(),
        P("head", None),
    )
    return jax.shard_map(
        on_device, mesh=mesh, in_specs=in_specs, out_specs=P("ctx", "head"), check_vma=False
    )
```

```python
import functools

import jax
import jax.numpy as jnp
from jax import lax
from jax.experimental import pallas as pl
from jax.experimental.pallas import tpu as pltpu
from jax.sharding import PartitionSpec as P

HD = 128
BLK = 8
NEG = -1e30
EXP2_SCALE = HD**-0.5 * 1.4426950408889634
FAR = -(1 << 20)
SAFE = 104.0
MIB = 1 << 20
VMEM = pltpu.VMEM
SMALL = pl.CostEstimate(flops=1 << 20, bytes_accessed=1 << 16, transcendentals=0)
LARGE = pl.CostEstimate(flops=1 << 34, bytes_accessed=1 << 27, transcendentals=0)


def shift(array, count, partner):
    pairs = [(i, partner(i)) for i in range(count)]
    return lax.ppermute(array, "ctx", [(i, j) for i, j in pairs if j is not None and 0 <= j < count])


def whole_vmem():
    return pl.BlockSpec(memory_space=VMEM)


def pack_body(ids, key_rows, values, queries, mine, send, sent_queries, keys, vals, sems, *, split):
    core = ids[0] % 2
    rows, width = keys.shape
    half = sent_queries.shape[1]
    theirs = pl.ds(pl.multiple_of((1 - core) * half, half), half)
    copies = [
        pltpu.make_async_copy(key_rows, keys, sems.at[0]),
        pltpu.make_async_copy(values, vals, sems.at[1]),
        pltpu.make_async_copy(queries.at[:, theirs], sent_queries, sems.at[2]),
    ]
    for copy in copies:
        copy.start()
    part = width // split
    copies[0].wait()
    for out, side in ((send, 1 - core), (mine, core)):
        first = pl.multiple_of(side * part if split == 2 else 0, HD)
        for r in range(0, rows, HD):
            for c in range(0, part, HD):
                out[r : r + HD, c : c + HD] = keys[r : r + HD, pl.ds(first + c, HD)].T
    copies[1].wait()
    for out, side in ((send, 1 - core), (mine, core)):
        first = pl.multiple_of(side * part if split == 2 else 0, HD)
        out[:, part:] = vals[:, pl.ds(first, part)]
    copies[2].wait()


def in_hbm(array):
    return pltpu.with_memory_space_constraint(array, pltpu.HBM)


def pack(ids, key_rows, values, queries, split):
    rows, width = key_rows.shape
    out = VMEM((rows, 2 * (width // split)), key_rows.dtype)
    return pl.pallas_call(
        functools.partial(pack_body, split=split),
        out_shape=[out, out, jax.ShapeDtypeStruct((rows, queries.shape[1] // 2), queries.dtype)],
        grid_spec=pltpu.PrefetchScalarGridSpec(
            num_scalar_prefetch=1,
            grid=(1,),
            in_specs=[pl.BlockSpec(memory_space=pl.ANY)] * 3,
            out_specs=[whole_vmem(), whole_vmem(), pl.BlockSpec(memory_space=pl.ANY)],
            scratch_shapes=[
                VMEM((rows, width), key_rows.dtype),
                VMEM((rows, width), key_rows.dtype),
                pltpu.SemaphoreType.DMA((3,)),
            ],
        ),
        compiler_params=pltpu.CompilerParams(vmem_limit_bytes=8 * MIB),
        name="pack",
    )(ids, in_hbm(key_rows), in_hbm(values), in_hbm(queries))


def join_body(ids, mine, other, own, upper):
    rows = mine.shape[0]
    core = ids[0] % 2
    own[pl.ds(pl.multiple_of(core * rows, rows), rows), :] = mine[...]
    own[pl.ds(pl.multiple_of((1 - core) * rows, rows), rows), :] = other[...]
    upper[...] = own[rows:, :]


def join(ids, mine, other):
    rows, width = mine.shape
    return pl.pallas_call(
        join_body,
        out_shape=[
            jax.ShapeDtypeStruct((2 * rows, width), mine.dtype),
            jax.ShapeDtypeStruct((rows, width), mine.dtype),
        ],
        grid_spec=pltpu.PrefetchScalarGridSpec(
            num_scalar_prefetch=1,
            grid=(1,),
            in_specs=[pl.BlockSpec((rows, width), lambda i, s: (0, 0))] * 2,
            out_specs=[
                pl.BlockSpec((2 * rows, width), lambda i, s: (0, 0)),
                pl.BlockSpec((rows, width), lambda i, s: (0, 0)),
            ],
        ),
        compiler_params=pltpu.CompilerParams(vmem_limit_bytes=8 * MIB),
        name="join",
    )(ids, mine, other)


def attend_body(*refs, spans, arrays, group, heads, which, first, fetch, carried, final):
    ids, lows, highs = refs[:3]
    q_own, q_got, start_ref = refs[3:6]
    refs = refs[6:]
    keys, vals, refs = refs[:arrays], refs[arrays : 2 * arrays], refs[2 * arrays + carried :]
    if fetch:
        weight, refs = refs[0], refs[1:]
    acc, top, reach = refs[:3]
    refs = refs[max(carried, 3) :]
    if fetch:
        held_weight, refs = refs[0], refs[1:]
    if final:
        out_ref, refs = refs[0], refs[1:]
    q, some_keys, some_values = refs[:3]

    here = ids[0]
    core, column = here % 2, here // 2 % 2
    rows = q_own.shape[0]
    h = pl.program_id(0)
    t = {"both": lambda: pl.program_id(1), "own": lambda: core, "other": lambda: 1 - core}[which]()
    chip_base = (here - core) * rows
    row_base = chip_base + t * rows
    least, greatest = lows[t], highs[t]

    if fetch:
        columns = held_weight.shape[1]
        first_column = pl.multiple_of(ids[2] * columns, 128)
        copy = pltpu.make_async_copy(weight.at[:, pl.ds(first_column, columns)], held_weight, refs[3])
        pl.when((h == 0) & (pl.program_id(1) == 0))(copy.start)

    bases = [base(chip_base, column, rows) for _, _, _, base in spans]
    runs = [(b + s[2] > least) & (b < row_base + rows) for b, s in zip(bases, spans)]
    fulls = [(b >= greatest) & (b + s[2] <= row_base + 1) for b, s in zip(bases, spans)]

    @pl.when(functools.reduce(jnp.logical_or, runs))
    def _():
        @pl.when(t == core)
        def _():
            for g in range(group):
                q[g] = q_own[:, g * HD : (g + 1) * HD]

        @pl.when(t != core)
        def _():
            for g in range(group):
                q[g] = q_got[:, g * HD : (g + 1) * HD]

    def turned(i):
        array, at, width, _ = spans[i]
        return jnp.concatenate([keys[array][r : r + HD, :] for r in range(at, at + width, HD)], axis=1)

    def with_ones(i):
        array, at, width, _ = spans[i]
        v = vals[array][at : at + width, :]
        return jnp.concatenate([v, jnp.ones((width, HD), v.dtype)], axis=1)

    def bias_of(base, width):
        key_pos = base + lax.broadcasted_iota(jnp.int32, (rows, width), 1)
        row_pos = row_base + lax.broadcasted_iota(jnp.int32, (rows, width), 0)
        starts = jnp.broadcast_to(start_ref[0].astype(jnp.float32), (HD, rows)).T
        starts = jnp.concatenate([starts] * (width // HD), axis=1)
        return jnp.where((key_pos <= row_pos) & (key_pos.astype(jnp.float32) >= starts), 0.0, NEG)

    def row_top(s):
        lane_top = s[:, :HD]
        for i in range(1, s.shape[1] // HD):
            lane_top = jnp.maximum(lane_top, s[:, i * HD : (i + 1) * HD])
        return jnp.max(lane_top, axis=1, keepdims=True)

    def weights_of(s, shift):
        wide = jnp.concatenate([shift] * (s.shape[1] // HD), axis=1)
        return jnp.exp2((s - wide) * EXP2_SCALE).astype(jnp.bfloat16)

    def step(kt, ve, base, mode, unroll):
        masked = base is not None
        if masked:
            bias = bias_of(base, kt.shape[1])

        def one_head(g, carry):
            q_here = q[g]
            s = jnp.dot(q_here, kt, preferred_element_type=jnp.float32)
            if masked:
                s = s + bias
            if mode == "first":
                m = jnp.broadcast_to(row_top(s), (rows, HD))
                top[h, t, g] = m
                acc[h, t, g] = jnp.dot(weights_of(s, m), ve, preferred_element_type=jnp.float32)
                sizes = jnp.abs(q_here.astype(jnp.float32))
                longest = jnp.maximum(carry[0], jnp.max(sizes.reshape(rows // 8, 8, HD), axis=0))
                lowest = jnp.minimum(carry[1], jnp.min(m.reshape(rows // 8, 8, HD), axis=0))
                return longest, lowest
            if mode == "kept":
                acc[h, t, g] += jnp.dot(weights_of(s, top[h, t, g]), ve, preferred_element_type=jnp.float32)
            else:
                m_old = top[h, t, g]
                m = jnp.maximum(m_old, row_top(s))
                fade = jnp.exp2((m_old - m) * EXP2_SCALE)
                update = jnp.dot(weights_of(s, m), ve, preferred_element_type=jnp.float32)
                top[h, t, g] = m
                acc[h, t, g] = acc[h, t, g] * jnp.concatenate([fade, fade], axis=1) + update
            return carry

        def some_heads(at, carry):
            for i in range(unroll):
                carry = one_head(at * unroll + i, carry)
            return carry

        carry = (jnp.zeros((8, HD), jnp.float32), jnp.full((8, HD), -NEG)) if mode == "first" else 0
        carry = lax.fori_loop(0, group // unroll, some_heads, carry)
        if mode == "first":
            reach[h, t, 0], reach[h, t, 1] = carry

    def all_keys(count):
        return jnp.concatenate([turned(i) for i in range(count)], axis=1)

    def all_values(count):
        return jnp.concatenate([with_ones(i) for i in range(count)], axis=0)

    count = len(spans)
    if first:
        pl.when(t == 0)(lambda: step(all_keys(1), all_values(1), bases[0], "first", group))
        pl.when(t == 1)(lambda: step(all_keys(count), all_values(count), bases[0], "first", group))
    else:
        room = jnp.min(reach[h, t, 1]) + SAFE / EXP2_SCALE
        widest = jnp.max(reach[h, t, 0], axis=0, keepdims=True)
        kt = all_keys(count).astype(jnp.float32)
        norms = jnp.max(jnp.sum(kt * kt, axis=0, keepdims=True), axis=1, keepdims=True)
        most = jnp.max(norms * jnp.sum(widest * widest, axis=1, keepdims=True)) * 1.01
        safe = (room > 0.0) & (most <= room * room)
        one_width = len({span[2] for span in spans}) == 1
        together = functools.reduce(jnp.logical_and, fulls) & safe if one_width else False
        if one_width:
            pl.when(together)(lambda: step(all_keys(count), all_values(count), None, "kept", group))

        def alone(chosen, width):
            def one_piece(piece, carry):
                choose = lambda options: functools.reduce(
                    lambda rest, i: jnp.where(piece == i, options[chosen[i]], rest),
                    range(1, len(chosen)),
                    options[chosen[0]],
                )
                base = choose(bases)
                run = choose([jnp.int32(r) for r in runs]) == 1

                @pl.when(run)
                def _():
                    for i, span in enumerate(chosen):

                        @pl.when(piece == i)
                        def _(span=span):
                            some_keys[:, :width] = turned(span)
                            some_values[:width] = with_ones(span)

                def part(base, mode, unroll):
                    return lambda: step(some_keys[:, :width], some_values[:width], base, mode, unroll)

                masked = run & safe
                if one_width:
                    full = choose([jnp.int32(f) for f in fulls]) == 1
                    pl.when(masked & full)(part(None, "kept", group))
                    masked = masked & jnp.logical_not(full)
                pl.when(masked)(part(base, "kept", group))
                pl.when(run & jnp.logical_not(safe))(part(base, "moved", 1))
                return carry

            lax.fori_loop(0, len(chosen), one_piece, 0)

        @pl.when(jnp.logical_not(together))
        def _():
            for width in sorted({span[2] for span in spans}):
                alone([i for i in range(count) if spans[i][2] == width], width)

    if fetch:
        pl.when((h == heads - 1) & (pl.program_id(1) == pl.num_programs(1) - 1))(copy.wait)
    if final:
        for g in range(group):
            a = acc[h, t, g]
            out_ref[:, g * HD : (g + 1) * HD] = (a[:, :HD] / a[:, HD:]).astype(jnp.bfloat16)


def attend(scalars, queries, got_queries, starts, pieces, spans, state, group, heads, which, weight=None, columns=0):
    rows, width = queries.shape[0], group * HD
    first, fetch, final = state is None, weight is not None, which != "both"
    tiles = 2 if which == "both" else 1

    def tile_of(t, ids):
        return {"both": t, "own": ids[0] % 2, "other": 1 - ids[0] % 2}[which]

    in_specs = [
        pl.BlockSpec((rows, width), lambda h, t, i, *_: (0, i[0] % 2 * heads + h)),
        pl.BlockSpec((rows, width), lambda h, t, *_: (0, h)),
        pl.BlockSpec((1, 1, rows), lambda h, t, i, *_: (tile_of(t, i), 0, 0)),
    ]
    in_specs += [pl.BlockSpec((p.shape[0], HD), lambda h, t, *_: (0, h)) for p in pieces]
    in_specs += [pl.BlockSpec((p.shape[0], HD), lambda h, t, *_: (0, heads + h)) for p in pieces]
    operands = [*scalars, in_hbm(queries), got_queries, starts, *pieces, *pieces]
    out_shape = [
        VMEM((heads, 2, group, rows, 2 * HD), jnp.float32),
        VMEM((heads, 2, group, rows, HD), jnp.float32),
        VMEM((heads, 2, 2, 8, HD), jnp.float32),
    ]
    aliases = {}
    if not first:
        out_shape = [VMEM(a.shape, a.dtype) for a in state]
        aliases = {len(operands) + i: i for i in range(len(state))}
        operands += state
        in_specs += [whole_vmem()] * len(state)
    out_specs = [whole_vmem()] * len(out_shape)
    wide = max(span[2] for span in spans)
    scratch = [
        VMEM((group, rows, HD), queries.dtype),
        VMEM((HD, wide), queries.dtype),
        VMEM((wide, 2 * HD), queries.dtype),
    ]
    if fetch:
        operands.append(weight)
        in_specs.append(pl.BlockSpec(memory_space=pl.ANY))
        out_shape.append(VMEM((weight.shape[0], columns), weight.dtype))
        out_specs.append(whole_vmem())
        scratch.append(pltpu.SemaphoreType.DMA)
    if final:
        out_shape.append(jax.ShapeDtypeStruct((rows, heads * width), queries.dtype))
        out_specs.append(pl.BlockSpec((rows, width), lambda h, t, *_: (0, h)))
    keys = sum(s[2] for s in spans)
    return pl.pallas_call(
        functools.partial(
            attend_body,
            spans=spans,
            arrays=len(pieces),
            group=group,
            heads=heads,
            which=which,
            first=first,
            fetch=fetch,
            carried=0 if first else len(state),
            final=final,
        ),
        out_shape=out_shape,
        grid_spec=pltpu.PrefetchScalarGridSpec(
            num_scalar_prefetch=3,
            grid=(heads, tiles),
            in_specs=in_specs,
            out_specs=out_specs,
            scratch_shapes=scratch,
        ),
        input_output_aliases=aliases,
        compiler_params=pltpu.CompilerParams(vmem_limit_bytes=14 * MIB),
        cost_estimate=SMALL,
        name=f"attend_{which}_{keys}",
    )(*operands)


def project_held_body(ids, a_ref, b_ref, w_ref, alias, o_ref, *, at, tile):
    half = a_ref.shape[1]
    core = ids[0] % 2
    mine = pl.ds(pl.multiple_of(core * half, half), half)
    theirs = pl.ds(pl.multiple_of((1 - core) * half, half), half)
    for n in range(o_ref.shape[1] // tile):
        cols = slice(at + n * tile, at + (n + 1) * tile)
        total = jnp.dot(a_ref[...], w_ref[mine, cols], preferred_element_type=jnp.float32)
        total = total + jnp.dot(b_ref[...], w_ref[theirs, cols], preferred_element_type=jnp.float32)
        o_ref[:, n * tile : (n + 1) * tile] = total.astype(o_ref.dtype)


def project_held(ids, a, b, held, at, columns):
    rows, half = a.shape
    block = lambda shape: pl.BlockSpec(shape, lambda i, s: (0, 0))
    return pl.pallas_call(
        functools.partial(project_held_body, at=at, tile=min(256, columns)),
        out_shape=[VMEM(held.shape, held.dtype), jax.ShapeDtypeStruct((rows, columns), a.dtype)],
        grid_spec=pltpu.PrefetchScalarGridSpec(
            num_scalar_prefetch=1,
            grid=(1,),
            in_specs=[block((rows, half)), block((rows, half)), whole_vmem()],
            out_specs=[whole_vmem(), block((rows, columns))],
        ),
        input_output_aliases={3: 0},
        compiler_params=pltpu.CompilerParams(vmem_limit_bytes=16 * MIB),
        cost_estimate=pl.CostEstimate(flops=4 * rows * half * columns, bytes_accessed=64 * MIB, transcendentals=0),
        name="project_held",
    )(ids, a, b, held)


def project_body(ids, a_ref, b_ref, wa_ref, wb_ref, o_ref):
    total = jnp.dot(a_ref[...], wa_ref[...], preferred_element_type=jnp.float32)
    total = total + jnp.dot(b_ref[...], wb_ref[...], preferred_element_type=jnp.float32)
    o_ref[...] = total.astype(o_ref.dtype)


def project(ids, a, b, weight, columns, at, chosen, tile):
    rows, half = a.shape
    first = lambda s: (s[1] * columns + at) // tile
    block = pl.BlockSpec((rows, half), lambda n, s: (0, 0))
    return pl.pallas_call(
        project_body,
        out_shape=jax.ShapeDtypeStruct((rows, chosen), a.dtype),
        grid_spec=pltpu.PrefetchScalarGridSpec(
            num_scalar_prefetch=1,
            grid=(chosen // tile,),
            in_specs=[
                block,
                block,
                pl.BlockSpec((half, tile), lambda n, s: (s[0] % 2, first(s) + n)),
                pl.BlockSpec((half, tile), lambda n, s: (1 - s[0] % 2, first(s) + n)),
            ],
            out_specs=pl.BlockSpec((rows, tile), lambda n, s: (0, n)),
        ),
        compiler_params=pltpu.CompilerParams(vmem_limit_bytes=48 * MIB),
        cost_estimate=LARGE if at else SMALL,
        name="project",
    )(ids, a, b, weight, weight)


def add_body(kept, arrived, *refs):
    refs[-1][...] = (kept[...].astype(jnp.float32) + arrived[...].astype(jnp.float32)).astype(refs[-1].dtype)


def add_columns(kept, arrived, columns, at, before):
    rows, tile = kept.shape[0], 512
    block = pl.BlockSpec((rows, tile), lambda n: (0, n))
    return pl.pallas_call(
        add_body,
        out_shape=jax.ShapeDtypeStruct((rows, columns), kept.dtype),
        grid=(kept.shape[1] // tile,),
        in_specs=[block, block] + [pl.BlockSpec(memory_space=pl.ANY)] * len(before),
        out_specs=pl.BlockSpec((rows, tile), lambda n: (0, at // tile + n)),
        input_output_aliases={2: 0} if before else {},
        compiler_params=pltpu.CompilerParams(vmem_limit_bytes=8 * MIB),
        cost_estimate=SMALL,
        name="add_columns",
    )(kept, arrived, *before)


def on_device(queries, key_rows, values, lengths, block_plan, inverse, mask_lo, out_weight):
    rows, query_width = queries.shape
    kv_heads = key_rows.shape[1] // HD
    count, head_count = lax.axis_size("ctx"), lax.axis_size("head")
    here, head_here = lax.axis_index("ctx"), lax.axis_index("head")
    core = here % 2
    split = 2 if kv_heads % 2 == 0 else 1
    heads = kv_heads // split
    half = query_width // 2
    group = half // (heads * HD)
    levels = count // 8

    place = jnp.arange(3, dtype=jnp.int32)
    send_half = 1 - head_here if head_count == 2 else 0
    ids = jnp.where(place == 0, here, jnp.where(place == 1, head_here, send_half)).astype(jnp.int32)

    sibling = functools.partial(shift, count=count, partner=lambda i: i ^ 1)
    mine, send, sent_queries = pack(ids, key_rows, values, queries, split)
    swapped = sibling(send)
    up_level = functools.partial(shift, count=count, partner=lambda i: i + 4)
    first_hop = [up_level(mine), up_level(swapped)]
    own, upper = join(ids, mine, swapped)
    sent_queries, lengths, mask_lo, _ = lax.optimization_barrier((sent_queries, lengths, mask_lo, swapped))
    got_queries = sibling(sent_queries)

    chip_base = (here - core) * rows
    doc_ends = jnp.cumsum(lengths)
    pos = chip_base + jnp.arange(2 * rows, dtype=jnp.int32)
    doc_start = jnp.max(jnp.where(doc_ends[None, :] <= pos[:, None], doc_ends[None, :], 0), axis=1)
    low = lax.dynamic_slice_in_dim(mask_lo, chip_base // BLK, 2 * rows // BLK) * BLK
    starts = jnp.maximum(doc_start, jnp.repeat(low, BLK)).astype(jnp.int32).reshape(2, rows)
    scalars = (ids, jnp.min(starts, axis=1), jnp.max(starts, axis=1))
    start_rows = starts[:, None, :]

    common = (scalars, queries, got_queries, start_rows)
    near = shift(own, count, lambda i: i + 2 if i // 2 % 2 == 0 else None)
    own_spans = [(0, 0, rows, lambda base, column, r: base), (0, rows, rows, lambda base, column, r: base + r)]
    state = attend(*common, [own], own_spans, None, group, heads, "both")
    keep = out_weight.shape[1] // head_count
    held_columns = keep if head_count == 2 else out_weight.shape[1]

    before, at_before = near, lambda base, column, r: jnp.where(column == 1, base - 2 * r, FAR)
    for d in range(1, levels + 1):
        if d == 1:
            first_hop = lax.optimization_barrier((*first_hop, state[2]))[:2]
            moving, _ = join(ids, *first_hop)
        else:
            moving, _ = lax.optimization_barrier((moving, state[2]))
        at_level = lambda base, column, r, d=d: base - 4 * d * r
        if d < levels:
            crossed = shift(moving, count, lambda i: i ^ 2)
            at_cross = lambda base, column, r, d=d: base - 4 * d * r + jnp.where(column == 0, 2 * r, -2 * r)
        else:
            crossed = shift(moving, count, lambda i: i - 2 if i // 2 % 2 == 1 else None)
            at_cross = lambda base, column, r, d=d: jnp.where(column == 0, base - 4 * d * r + 2 * r, FAR)
        onward = shift(moving, count, lambda i: i + 4) if d < levels else None
        if d == 1:
            reach = 4 * levels + 2
            upper, _ = lax.optimization_barrier((upper, moving))
            farthest = shift(upper, count, lambda i: i + reach)
        spans = [(0, 0, 2 * rows, at_before), (1, 0, 2 * rows, at_level)]
        fetch = (out_weight, held_columns) if d == levels else ()
        state = attend(*common, [before, moving], spans, state, group, heads, "both", *fetch)
        before, at_before, moving = crossed, at_cross, onward
    at_farthest = lambda base, column, r: base - reach * r + r
    spans = [(0, 0, 2 * rows, at_before), (1, 0, rows, at_farthest)]
    *state, theirs = attend(*common, [before, farthest], spans, state, group, heads, "other")
    got = sibling(theirs)
    *state, att = attend(*common, [before, farthest], spans, state, group, heads, "own")
    held = state[3]

    if head_count != 2:
        _, partial_sums = project_held(ids, att, got, held, 0, held_columns)
        return lax.psum_scatter(partial_sums, "head", scatter_dimension=1, tiled=True)
    parts = ((0, keep // 4), (keep // 4, keep // 2), (3 * keep // 4, keep // 4))
    arrived = []
    for at, columns in parts:
        held, sent = project_held(ids, att, got, held, at, columns)
        arrived.append(lax.ppermute(sent, "head", [(0, 1), (1, 0)]))
    out = []
    for (at, columns), part in zip(parts, arrived):
        kept = project(ids, att, got, out_weight, keep, at, columns, 256)
        out = [add_columns(kept, part, keep, at, out)]
        ids, _ = lax.optimization_barrier((ids, out[0]))
    return out[0]


def solution(mesh):
    in_specs = (
        P("ctx", "head"),
        P("ctx", "head"),
        P("ctx", "head"),
        P(),
        P("ctx"),
        P(),
        P(),
        P("head", None),
    )
    return jax.shard_map(
        on_device, mesh=mesh, in_specs=in_specs, out_specs=P("ctx", "head"), check_vma=False
    )
```

```python
import functools

import jax
import jax.numpy as jnp
from jax import lax
from jax.experimental import pallas as pl
from jax.experimental.pallas import tpu as pltpu
from jax.sharding import PartitionSpec as P

HD = 128
BLK = 8
NEG = -1e30
EXP2_SCALE = HD**-0.5 * 1.4426950408889634
FAR = -(1 << 20)
SAFE = 104.0
MIB = 1 << 20
VMEM = pltpu.VMEM
SMALL = pl.CostEstimate(flops=1 << 20, bytes_accessed=1 << 16, transcendentals=0)
LARGE = pl.CostEstimate(flops=1 << 34, bytes_accessed=1 << 27, transcendentals=0)


def shift(array, count, partner):
    pairs = [(i, partner(i)) for i in range(count)]
    return lax.ppermute(array, "ctx", [(i, j) for i, j in pairs if j is not None and 0 <= j < count])


def whole_vmem():
    return pl.BlockSpec(memory_space=VMEM)


def pack_body(ids, key_rows, values, queries, mine, send, sent_queries, keys, vals, sems, *, split):
    core = ids[0] % 2
    rows, width = keys.shape
    half = sent_queries.shape[1]
    theirs = pl.ds(pl.multiple_of((1 - core) * half, half), half)
    copies = [
        pltpu.make_async_copy(key_rows, keys, sems.at[0]),
        pltpu.make_async_copy(values, vals, sems.at[1]),
        pltpu.make_async_copy(queries.at[:, theirs], sent_queries, sems.at[2]),
    ]
    for copy in copies:
        copy.start()
    part = width // split
    copies[0].wait()
    for out, side in ((send, 1 - core), (mine, core)):
        first = pl.multiple_of(side * part if split == 2 else 0, HD)
        for r in range(0, rows, HD):
            for c in range(0, part, HD):
                out[r : r + HD, c : c + HD] = keys[r : r + HD, pl.ds(first + c, HD)].T
    copies[1].wait()
    for out, side in ((send, 1 - core), (mine, core)):
        first = pl.multiple_of(side * part if split == 2 else 0, HD)
        out[:, part:] = vals[:, pl.ds(first, part)]
    copies[2].wait()


def in_hbm(array):
    return pltpu.with_memory_space_constraint(array, pltpu.HBM)


def pack(ids, key_rows, values, queries, split):
    rows, width = key_rows.shape
    out = VMEM((rows, 2 * (width // split)), key_rows.dtype)
    return pl.pallas_call(
        functools.partial(pack_body, split=split),
        out_shape=[out, out, jax.ShapeDtypeStruct((rows, queries.shape[1] // 2), queries.dtype)],
        grid_spec=pltpu.PrefetchScalarGridSpec(
            num_scalar_prefetch=1,
            grid=(1,),
            in_specs=[pl.BlockSpec(memory_space=pl.ANY)] * 3,
            out_specs=[whole_vmem(), whole_vmem(), pl.BlockSpec(memory_space=pl.ANY)],
            scratch_shapes=[
                VMEM((rows, width), key_rows.dtype),
                VMEM((rows, width), key_rows.dtype),
                pltpu.SemaphoreType.DMA((3,)),
            ],
        ),
        compiler_params=pltpu.CompilerParams(vmem_limit_bytes=8 * MIB),
        name="pack",
    )(ids, in_hbm(key_rows), in_hbm(values), in_hbm(queries))


def join_body(ids, mine, other, own, upper):
    rows = mine.shape[0]
    core = ids[0] % 2
    own[pl.ds(pl.multiple_of(core * rows, rows), rows), :] = mine[...]
    own[pl.ds(pl.multiple_of((1 - core) * rows, rows), rows), :] = other[...]
    upper[...] = own[rows:, :]


def join(ids, mine, other):
    rows, width = mine.shape
    return pl.pallas_call(
        join_body,
        out_shape=[
            jax.ShapeDtypeStruct((2 * rows, width), mine.dtype),
            jax.ShapeDtypeStruct((rows, width), mine.dtype),
        ],
        grid_spec=pltpu.PrefetchScalarGridSpec(
            num_scalar_prefetch=1,
            grid=(1,),
            in_specs=[pl.BlockSpec((rows, width), lambda i, s: (0, 0))] * 2,
            out_specs=[
                pl.BlockSpec((2 * rows, width), lambda i, s: (0, 0)),
                pl.BlockSpec((rows, width), lambda i, s: (0, 0)),
            ],
        ),
        compiler_params=pltpu.CompilerParams(vmem_limit_bytes=8 * MIB),
        name="join",
    )(ids, mine, other)


def attend_body(*refs, q_count, spans, arrays, group, heads, which, first, fetch, carried, final):
    ids, lows, highs = refs[:3]
    sources, start_ref = refs[3 : 3 + q_count], refs[3 + q_count]
    refs = refs[4 + q_count :]
    keys, vals, refs = refs[:arrays], refs[arrays : 2 * arrays], refs[2 * arrays + carried :]
    if fetch:
        weight, refs = refs[0], refs[1:]
    acc, top, reach = refs[:3]
    refs = refs[max(carried, 3) :]
    if fetch:
        held_weight, refs = refs[0], refs[1:]
    if final:
        out_ref, refs = refs[0], refs[1:]
    q, some_keys, some_values = refs[:3]

    here = ids[0]
    core, column = here % 2, here // 2 % 2
    rows = sources[0].shape[0]
    h = pl.program_id(0)
    t = {"both": lambda: pl.program_id(1), "own": lambda: core, "other": lambda: 1 - core}[which]()
    chip_base = (here - core) * rows
    row_base = chip_base + t * rows
    least, greatest = lows[t], highs[t]

    if fetch:
        columns = held_weight.shape[1]
        first_column = pl.multiple_of(ids[2] * columns, 128)
        copy = pltpu.make_async_copy(weight.at[:, pl.ds(first_column, columns)], held_weight, refs[3])
        pl.when((h == 0) & (pl.program_id(1) == 0))(copy.start)

    bases = [base(chip_base, column, rows) for _, _, _, base in spans]
    runs = [(b + s[2] > least) & (b < row_base + rows) for b, s in zip(bases, spans)]
    fulls = [(b >= greatest) & (b + s[2] <= row_base + 1) for b, s in zip(bases, spans)]

    @pl.when(functools.reduce(jnp.logical_or, runs))
    def _():
        for i, source in enumerate(sources):
            here_or_there = (t == core) == (i == 0) if q_count == 2 else True

            @pl.when(here_or_there)
            def _(source=source):
                for g in range(group):
                    q[g] = source[:, g * HD : (g + 1) * HD]

    def turned(i):
        array, at, width, _ = spans[i]
        return jnp.concatenate([keys[array][r : r + HD, :] for r in range(at, at + width, HD)], axis=1)

    def with_ones(i):
        array, at, width, _ = spans[i]
        v = vals[array][at : at + width, :]
        return jnp.concatenate([v, jnp.ones((width, HD), v.dtype)], axis=1)

    def bias_of(base, width):
        key_pos = base + lax.broadcasted_iota(jnp.int32, (rows, width), 1)
        row_pos = row_base + lax.broadcasted_iota(jnp.int32, (rows, width), 0)
        starts = jnp.broadcast_to(start_ref[0].astype(jnp.float32), (HD, rows)).T
        starts = jnp.concatenate([starts] * (width // HD), axis=1)
        return jnp.where((key_pos <= row_pos) & (key_pos.astype(jnp.float32) >= starts), 0.0, NEG)

    def row_top(s):
        lane_top = s[:, :HD]
        for i in range(1, s.shape[1] // HD):
            lane_top = jnp.maximum(lane_top, s[:, i * HD : (i + 1) * HD])
        return jnp.max(lane_top, axis=1, keepdims=True)

    def weights_of(s, shift):
        wide = jnp.concatenate([shift] * (s.shape[1] // HD), axis=1)
        return jnp.exp2((s - wide) * EXP2_SCALE).astype(jnp.bfloat16)

    def step(kt, ve, base, mode, unroll):
        masked = base is not None
        if masked:
            bias = bias_of(base, kt.shape[1])

        def one_head(g, carry):
            q_here = q[g]
            s = jnp.dot(q_here, kt, preferred_element_type=jnp.float32)
            if masked:
                s = s + bias
            if mode == "first":
                m = jnp.broadcast_to(row_top(s), (rows, HD))
                top[h, t, g] = m
                acc[h, t, g] = jnp.dot(weights_of(s, m), ve, preferred_element_type=jnp.float32)
                sizes = jnp.abs(q_here.astype(jnp.float32))
                longest = jnp.maximum(carry[0], jnp.max(sizes.reshape(rows // 8, 8, HD), axis=0))
                lowest = jnp.minimum(carry[1], jnp.min(m.reshape(rows // 8, 8, HD), axis=0))
                return longest, lowest
            if mode == "kept":
                acc[h, t, g] += jnp.dot(weights_of(s, top[h, t, g]), ve, preferred_element_type=jnp.float32)
            else:
                m_old = top[h, t, g]
                m = jnp.maximum(m_old, row_top(s))
                fade = jnp.exp2((m_old - m) * EXP2_SCALE)
                update = jnp.dot(weights_of(s, m), ve, preferred_element_type=jnp.float32)
                top[h, t, g] = m
                acc[h, t, g] = acc[h, t, g] * jnp.concatenate([fade, fade], axis=1) + update
            return carry

        def some_heads(at, carry):
            for i in range(unroll):
                carry = one_head(at * unroll + i, carry)
            return carry

        carry = (jnp.zeros((8, HD), jnp.float32), jnp.full((8, HD), -NEG)) if mode == "first" else 0
        carry = lax.fori_loop(0, group // unroll, some_heads, carry)
        if mode == "first":
            reach[h, t, 0], reach[h, t, 1] = carry

    def all_keys(count):
        return jnp.concatenate([turned(i) for i in range(count)], axis=1)

    def all_values(count):
        return jnp.concatenate([with_ones(i) for i in range(count)], axis=0)

    count = len(spans)
    if first:
        pl.when(t == 0)(lambda: step(all_keys(1), all_values(1), bases[0], "first", group))
        pl.when(t == 1)(lambda: step(all_keys(count), all_values(count), bases[0], "first", group))
    else:
        room = jnp.min(reach[h, t, 1]) + SAFE / EXP2_SCALE
        widest = jnp.max(reach[h, t, 0], axis=0, keepdims=True)
        kt = all_keys(count).astype(jnp.float32)
        norms = jnp.max(jnp.sum(kt * kt, axis=0, keepdims=True), axis=1, keepdims=True)
        most = jnp.max(norms * jnp.sum(widest * widest, axis=1, keepdims=True)) * 1.01
        safe = (room > 0.0) & (most <= room * room)
        one_width = len({span[2] for span in spans}) == 1
        together = functools.reduce(jnp.logical_and, fulls) & safe if one_width else False
        if one_width:
            pl.when(together)(lambda: step(all_keys(count), all_values(count), None, "kept", group))

        def alone(chosen, width):
            def one_piece(piece, carry):
                choose = lambda options: functools.reduce(
                    lambda rest, i: jnp.where(piece == i, options[chosen[i]], rest),
                    range(1, len(chosen)),
                    options[chosen[0]],
                )
                base = choose(bases)
                run = choose([jnp.int32(r) for r in runs]) == 1

                @pl.when(run)
                def _():
                    for i, span in enumerate(chosen):

                        @pl.when(piece == i)
                        def _(span=span):
                            some_keys[:, :width] = turned(span)
                            some_values[:width] = with_ones(span)

                def part(base, mode, unroll):
                    return lambda: step(some_keys[:, :width], some_values[:width], base, mode, unroll)

                masked = run & safe
                if one_width:
                    full = choose([jnp.int32(f) for f in fulls]) == 1
                    pl.when(masked & full)(part(None, "kept", group))
                    masked = masked & jnp.logical_not(full)
                pl.when(masked)(part(base, "kept", group))
                pl.when(run & jnp.logical_not(safe))(part(base, "moved", 1))
                return carry

            lax.fori_loop(0, len(chosen), one_piece, 0)

        @pl.when(jnp.logical_not(together))
        def _():
            for width in sorted({span[2] for span in spans}):
                alone([i for i in range(count) if spans[i][2] == width], width)

    if fetch:
        pl.when((h == heads - 1) & (pl.program_id(1) == pl.num_programs(1) - 1))(copy.wait)
    if final:
        for g in range(group):
            a = acc[h, t, g]
            out_ref[:, g * HD : (g + 1) * HD] = (a[:, :HD] / a[:, HD:]).astype(jnp.bfloat16)


def attend(scalars, queries, got_queries, starts, pieces, spans, state, group, heads, which, weight=None, columns=0):
    rows, width = queries.shape[0], group * HD
    first, fetch, final = state is None, weight is not None, which != "both"
    tiles = 2 if which == "both" else 1

    def tile_of(t, ids):
        return {"both": t, "own": ids[0] % 2, "other": 1 - ids[0] % 2}[which]

    own_queries = (in_hbm(queries), pl.BlockSpec((rows, width), lambda h, t, i, *_: (0, i[0] % 2 * heads + h)))
    other_queries = (got_queries, pl.BlockSpec((rows, width), lambda h, t, *_: (0, h)))
    sources = {"both": [own_queries, other_queries], "own": [own_queries], "other": [other_queries]}[which]
    in_specs = [spec for _, spec in sources]
    in_specs.append(pl.BlockSpec((1, 1, rows), lambda h, t, i, *_: (tile_of(t, i), 0, 0)))
    in_specs += [pl.BlockSpec((p.shape[0], HD), lambda h, t, *_: (0, h)) for p in pieces]
    in_specs += [pl.BlockSpec((p.shape[0], HD), lambda h, t, *_: (0, heads + h)) for p in pieces]
    operands = [*scalars, *(array for array, _ in sources), starts, *pieces, *pieces]
    out_shape = [
        VMEM((heads, 2, group, rows, 2 * HD), jnp.float32),
        VMEM((heads, 2, group, rows, HD), jnp.float32),
        VMEM((heads, 2, 2, 8, HD), jnp.float32),
    ]
    aliases = {}
    if not first:
        out_shape = [VMEM(a.shape, a.dtype) for a in state]
        aliases = {len(operands) + i: i for i in range(len(state))}
        operands += state
        in_specs += [whole_vmem()] * len(state)
    out_specs = [whole_vmem()] * len(out_shape)
    wide = max(span[2] for span in spans)
    scratch = [
        VMEM((group, rows, HD), queries.dtype),
        VMEM((HD, wide), queries.dtype),
        VMEM((wide, 2 * HD), queries.dtype),
    ]
    if fetch:
        operands.append(weight)
        in_specs.append(pl.BlockSpec(memory_space=pl.ANY))
        out_shape.append(VMEM((weight.shape[0], columns), weight.dtype))
        out_specs.append(whole_vmem())
        scratch.append(pltpu.SemaphoreType.DMA)
    if final:
        out_shape.append(jax.ShapeDtypeStruct((rows, heads * width), queries.dtype))
        out_specs.append(pl.BlockSpec((rows, width), lambda h, t, *_: (0, h)))
    keys = sum(s[2] for s in spans)
    return pl.pallas_call(
        functools.partial(
            attend_body,
            q_count=len(sources),
            spans=spans,
            arrays=len(pieces),
            group=group,
            heads=heads,
            which=which,
            first=first,
            fetch=fetch,
            carried=0 if first else len(state),
            final=final,
        ),
        out_shape=out_shape,
        grid_spec=pltpu.PrefetchScalarGridSpec(
            num_scalar_prefetch=3,
            grid=(heads, tiles),
            in_specs=in_specs,
            out_specs=out_specs,
            scratch_shapes=scratch,
        ),
        input_output_aliases=aliases,
        compiler_params=pltpu.CompilerParams(vmem_limit_bytes=14 * MIB),
        cost_estimate=SMALL,
        name=f"attend_{which}_{keys}",
    )(*operands)


def project_held_body(ids, a_ref, b_ref, w_ref, alias, o_ref, *, at, tile):
    half = a_ref.shape[1]
    core = ids[0] % 2
    mine = pl.ds(pl.multiple_of(core * half, half), half)
    theirs = pl.ds(pl.multiple_of((1 - core) * half, half), half)
    for n in range(o_ref.shape[1] // tile):
        cols = slice(at + n * tile, at + (n + 1) * tile)
        total = jnp.dot(a_ref[...], w_ref[mine, cols], preferred_element_type=jnp.float32)
        total = total + jnp.dot(b_ref[...], w_ref[theirs, cols], preferred_element_type=jnp.float32)
        o_ref[:, n * tile : (n + 1) * tile] = total.astype(o_ref.dtype)


def project_held(ids, a, b, held, at, columns):
    rows, half = a.shape
    block = lambda shape: pl.BlockSpec(shape, lambda i, s: (0, 0))
    return pl.pallas_call(
        functools.partial(project_held_body, at=at, tile=min(256, columns)),
        out_shape=[VMEM(held.shape, held.dtype), jax.ShapeDtypeStruct((rows, columns), a.dtype)],
        grid_spec=pltpu.PrefetchScalarGridSpec(
            num_scalar_prefetch=1,
            grid=(1,),
            in_specs=[block((rows, half)), block((rows, half)), whole_vmem()],
            out_specs=[whole_vmem(), block((rows, columns))],
        ),
        input_output_aliases={3: 0},
        compiler_params=pltpu.CompilerParams(vmem_limit_bytes=16 * MIB),
        cost_estimate=pl.CostEstimate(flops=4 * rows * half * columns, bytes_accessed=64 * MIB, transcendentals=0),
        name="project_held",
    )(ids, a, b, held)


def project_body(ids, a_ref, b_ref, wa_ref, wb_ref, o_ref):
    total = jnp.dot(a_ref[...], wa_ref[...], preferred_element_type=jnp.float32)
    total = total + jnp.dot(b_ref[...], wb_ref[...], preferred_element_type=jnp.float32)
    o_ref[...] = total.astype(o_ref.dtype)


def project(ids, a, b, weight, columns, at, chosen, tile):
    rows, half = a.shape
    first = lambda s: (s[1] * columns + at) // tile
    block = pl.BlockSpec((rows, half), lambda n, s: (0, 0))
    return pl.pallas_call(
        project_body,
        out_shape=jax.ShapeDtypeStruct((rows, chosen), a.dtype),
        grid_spec=pltpu.PrefetchScalarGridSpec(
            num_scalar_prefetch=1,
            grid=(chosen // tile,),
            in_specs=[
                block,
                block,
                pl.BlockSpec((half, tile), lambda n, s: (s[0] % 2, first(s) + n)),
                pl.BlockSpec((half, tile), lambda n, s: (1 - s[0] % 2, first(s) + n)),
            ],
            out_specs=pl.BlockSpec((rows, tile), lambda n, s: (0, n)),
        ),
        compiler_params=pltpu.CompilerParams(vmem_limit_bytes=48 * MIB),
        cost_estimate=LARGE if at else SMALL,
        name="project",
    )(ids, a, b, weight, weight)


def add_body(kept, arrived, *refs):
    refs[-1][...] = (kept[...].astype(jnp.float32) + arrived[...].astype(jnp.float32)).astype(refs[-1].dtype)


def add_columns(kept, arrived, columns, at, before):
    rows, tile = kept.shape[0], 512
    block = pl.BlockSpec((rows, tile), lambda n: (0, n))
    return pl.pallas_call(
        add_body,
        out_shape=jax.ShapeDtypeStruct((rows, columns), kept.dtype),
        grid=(kept.shape[1] // tile,),
        in_specs=[block, block] + [pl.BlockSpec(memory_space=pl.ANY)] * len(before),
        out_specs=pl.BlockSpec((rows, tile), lambda n: (0, at // tile + n)),
        input_output_aliases={2: 0} if before else {},
        compiler_params=pltpu.CompilerParams(vmem_limit_bytes=8 * MIB),
        cost_estimate=SMALL,
        name="add_columns",
    )(kept, arrived, *before)


def on_device(queries, key_rows, values, lengths, block_plan, inverse, mask_lo, out_weight):
    rows, query_width = queries.shape
    kv_heads = key_rows.shape[1] // HD
    count, head_count = lax.axis_size("ctx"), lax.axis_size("head")
    here, head_here = lax.axis_index("ctx"), lax.axis_index("head")
    core = here % 2
    split = 2 if kv_heads % 2 == 0 else 1
    heads = kv_heads // split
    half = query_width // 2
    group = half // (heads * HD)
    levels = count // 8

    place = jnp.arange(3, dtype=jnp.int32)
    send_half = 1 - head_here if head_count == 2 else 0
    ids = jnp.where(place == 0, here, jnp.where(place == 1, head_here, send_half)).astype(jnp.int32)

    sibling = functools.partial(shift, count=count, partner=lambda i: i ^ 1)
    mine, send, sent_queries = pack(ids, key_rows, values, queries, split)
    swapped = sibling(send)
    lengths, mask_lo, _ = lax.optimization_barrier((lengths, mask_lo, send))
    chip_base = (here - core) * rows
    doc_ends = jnp.cumsum(lengths)
    pos = chip_base + jnp.arange(2 * rows, dtype=jnp.int32)
    doc_start = jnp.max(jnp.where(doc_ends[None, :] <= pos[:, None], doc_ends[None, :], 0), axis=1)
    low = lax.dynamic_slice_in_dim(mask_lo, chip_base // BLK, 2 * rows // BLK) * BLK
    starts = jnp.maximum(doc_start, jnp.repeat(low, BLK)).astype(jnp.int32).reshape(2, rows)
    scalars = (ids, jnp.min(starts, axis=1), jnp.max(starts, axis=1))
    start_rows = starts[:, None, :]
    swapped, start_rows, lows, highs = lax.optimization_barrier((swapped, start_rows, *scalars[1:]))
    scalars = (ids, lows, highs)

    up_level = functools.partial(shift, count=count, partner=lambda i: i + 4)
    first_hop = [up_level(mine), up_level(swapped)]
    own, upper = join(ids, mine, swapped)
    sent_queries, _ = lax.optimization_barrier((sent_queries, swapped))
    got_queries = sibling(sent_queries)

    common = (scalars, queries, got_queries, start_rows)
    near = shift(own, count, lambda i: i + 2 if i // 2 % 2 == 0 else None)
    own_spans = [(0, 0, rows, lambda base, column, r: base), (0, rows, rows, lambda base, column, r: base + r)]
    state = attend(*common, [own], own_spans, None, group, heads, "both")
    keep = out_weight.shape[1] // head_count
    held_columns = keep if head_count == 2 else out_weight.shape[1]

    before, at_before = near, lambda base, column, r: jnp.where(column == 1, base - 2 * r, FAR)
    for d in range(1, levels + 1):
        if d == 1:
            first_hop = lax.optimization_barrier((*first_hop, state[2]))[:2]
            moving, _ = join(ids, *first_hop)
        else:
            moving, _ = lax.optimization_barrier((moving, state[2]))
        at_level = lambda base, column, r, d=d: base - 4 * d * r
        if d < levels:
            crossed = shift(moving, count, lambda i: i ^ 2)
            at_cross = lambda base, column, r, d=d: base - 4 * d * r + jnp.where(column == 0, 2 * r, -2 * r)
        else:
            crossed = shift(moving, count, lambda i: i - 2 if i // 2 % 2 == 1 else None)
            at_cross = lambda base, column, r, d=d: jnp.where(column == 0, base - 4 * d * r + 2 * r, FAR)
        onward = shift(moving, count, lambda i: i + 4) if d < levels else None
        if d == 1:
            reach = 4 * levels + 2
            upper, _ = lax.optimization_barrier((upper, moving))
            farthest = shift(upper, count, lambda i: i + reach)
        spans = [(0, 0, 2 * rows, at_before), (1, 0, 2 * rows, at_level)]
        fetch = (out_weight, held_columns) if d == 1 else ()
        state = attend(*common, [before, moving], spans, state, group, heads, "both", *fetch)
        before, at_before, moving = crossed, at_cross, onward
    at_farthest = lambda base, column, r: base - reach * r + r
    spans = [(0, 0, 2 * rows, at_before), (1, 0, rows, at_farthest)]
    *state, theirs = attend(*common, [before, farthest], spans, state, group, heads, "other")
    got = sibling(theirs)
    *state, att = attend(*common, [before, farthest], spans, state, group, heads, "own")
    held = state[3]

    if head_count != 2:
        _, partial_sums = project_held(ids, att, got, held, 0, held_columns)
        return lax.psum_scatter(partial_sums, "head", scatter_dimension=1, tiled=True)
    parts = ((0, keep // 4), (keep // 4, keep // 2), (3 * keep // 4, keep // 4))
    arrived = []
    for at, columns in parts:
        held, sent = project_held(ids, att, got, held, at, columns)
        arrived.append(lax.ppermute(sent, "head", [(0, 1), (1, 0)]))
    out = []
    for (at, columns), part in zip(parts, arrived):
        kept = project(ids, att, got, out_weight, keep, at, columns, 256)
        out = [add_columns(kept, part, keep, at, out)]
        ids, _ = lax.optimization_barrier((ids, out[0]))
    return out[0]


def solution(mesh):
    in_specs = (
        P("ctx", "head"),
        P("ctx", "head"),
        P("ctx", "head"),
        P(),
        P("ctx"),
        P(),
        P(),
        P("head", None),
    )
    return jax.shard_map(
        on_device, mesh=mesh, in_specs=in_specs, out_specs=P("ctx", "head"), check_vma=False
    )
```

```python
import functools

import jax
import jax.numpy as jnp
from jax import lax
from jax.experimental import pallas as pl
from jax.experimental.pallas import tpu as pltpu
from jax.sharding import PartitionSpec as P

HD = 128
BLK = 8
NEG = -1e30
EXP2_SCALE = HD**-0.5 * 1.4426950408889634
FAR = -(1 << 20)
SAFE = 104.0
MIB = 1 << 20
VMEM = pltpu.VMEM
SMALL = pl.CostEstimate(flops=1 << 20, bytes_accessed=1 << 16, transcendentals=0)
LARGE = pl.CostEstimate(flops=1 << 34, bytes_accessed=1 << 27, transcendentals=0)


def shift(array, count, partner):
    pairs = [(i, partner(i)) for i in range(count)]
    return lax.ppermute(array, "ctx", [(i, j) for i, j in pairs if j is not None and 0 <= j < count])


def whole_vmem():
    return pl.BlockSpec(memory_space=VMEM)


def pack_body(ids, key_rows, values, queries, mine, send, kept_queries, sent_queries, keys, vals, sems, *, split):
    core = ids[0] % 2
    rows, width = keys.shape
    half = sent_queries.shape[1]
    ours = pl.ds(pl.multiple_of(core * half, half), half)
    theirs = pl.ds(pl.multiple_of((1 - core) * half, half), half)
    copies = [
        pltpu.make_async_copy(key_rows, keys, sems.at[0]),
        pltpu.make_async_copy(values, vals, sems.at[1]),
        pltpu.make_async_copy(queries.at[:, theirs], sent_queries, sems.at[2]),
        pltpu.make_async_copy(queries.at[:, ours], kept_queries, sems.at[3]),
    ]
    for copy in copies:
        copy.start()
    part = width // split
    copies[0].wait()
    for out, side in ((send, 1 - core), (mine, core)):
        first = pl.multiple_of(side * part if split == 2 else 0, HD)
        for r in range(0, rows, HD):
            for c in range(0, part, HD):
                out[r : r + HD, c : c + HD] = keys[r : r + HD, pl.ds(first + c, HD)].T
    copies[1].wait()
    for out, side in ((send, 1 - core), (mine, core)):
        first = pl.multiple_of(side * part if split == 2 else 0, HD)
        out[:, part:] = vals[:, pl.ds(first, part)]
    copies[2].wait()
    copies[3].wait()


def in_hbm(array):
    return pltpu.with_memory_space_constraint(array, pltpu.HBM)


def pack(ids, key_rows, values, queries, split):
    rows, width = key_rows.shape
    out = VMEM((rows, 2 * (width // split)), key_rows.dtype)
    return pl.pallas_call(
        functools.partial(pack_body, split=split),
        out_shape=[out, out] + [VMEM((rows, queries.shape[1] // 2), queries.dtype)] * 2,
        grid_spec=pltpu.PrefetchScalarGridSpec(
            num_scalar_prefetch=1,
            grid=(1,),
            in_specs=[pl.BlockSpec(memory_space=pl.ANY)] * 3,
            out_specs=[whole_vmem()] * 4,
            scratch_shapes=[
                VMEM((rows, width), key_rows.dtype),
                VMEM((rows, width), key_rows.dtype),
                pltpu.SemaphoreType.DMA((4,)),
            ],
        ),
        compiler_params=pltpu.CompilerParams(vmem_limit_bytes=8 * MIB),
        name="pack",
    )(ids, in_hbm(key_rows), in_hbm(values), in_hbm(queries))


def join_body(ids, mine, other, own, upper):
    rows = mine.shape[0]
    core = ids[0] % 2
    own[pl.ds(pl.multiple_of(core * rows, rows), rows), :] = mine[...]
    own[pl.ds(pl.multiple_of((1 - core) * rows, rows), rows), :] = other[...]
    upper[...] = own[rows:, :]


def join(ids, mine, other):
    rows, width = mine.shape
    return pl.pallas_call(
        join_body,
        out_shape=[
            jax.ShapeDtypeStruct((2 * rows, width), mine.dtype),
            jax.ShapeDtypeStruct((rows, width), mine.dtype),
        ],
        grid_spec=pltpu.PrefetchScalarGridSpec(
            num_scalar_prefetch=1,
            grid=(1,),
            in_specs=[pl.BlockSpec((rows, width), lambda i, s: (0, 0))] * 2,
            out_specs=[
                pl.BlockSpec((2 * rows, width), lambda i, s: (0, 0)),
                pl.BlockSpec((rows, width), lambda i, s: (0, 0)),
            ],
        ),
        compiler_params=pltpu.CompilerParams(vmem_limit_bytes=8 * MIB),
        name="join",
    )(ids, mine, other)


def attend_body(*refs, q_count, spans, arrays, group, heads, which, first, fetch, carried, final):
    ids, lows, highs = refs[:3]
    sources, start_ref = refs[3 : 3 + q_count], refs[3 + q_count]
    refs = refs[4 + q_count :]
    keys, vals, refs = refs[:arrays], refs[arrays : 2 * arrays], refs[2 * arrays + carried :]
    if fetch:
        weight, refs = refs[0], refs[1:]
    acc, top, reach = refs[:3]
    refs = refs[max(carried, 3) :]
    if fetch:
        held_weight, refs = refs[0], refs[1:]
    if final:
        out_ref, refs = refs[0], refs[1:]
    q, some_keys, some_values = refs[:3]

    here = ids[0]
    core, column = here % 2, here // 2 % 2
    rows = sources[0].shape[0]
    h = pl.program_id(0)
    t = {"both": lambda: pl.program_id(1), "own": lambda: core, "other": lambda: 1 - core}[which]()
    chip_base = (here - core) * rows
    row_base = chip_base + t * rows
    least, greatest = lows[t], highs[t]

    if fetch:
        columns = held_weight.shape[1]
        first_column = pl.multiple_of(ids[2] * columns, 128)
        copy = pltpu.make_async_copy(weight.at[:, pl.ds(first_column, columns)], held_weight, refs[3])
        pl.when((h == 0) & (pl.program_id(1) == 0))(copy.start)

    bases = [base(chip_base, column, rows) for _, _, _, base in spans]
    runs = [(b + s[2] > least) & (b < row_base + rows) for b, s in zip(bases, spans)]
    fulls = [(b >= greatest) & (b + s[2] <= row_base + 1) for b, s in zip(bases, spans)]

    @pl.when(functools.reduce(jnp.logical_or, runs))
    def _():
        for i, source in enumerate(sources):
            here_or_there = (t == core) == (i == 0) if q_count == 2 else True

            @pl.when(here_or_there)
            def _(source=source):
                for g in range(group):
                    q[g] = source[:, g * HD : (g + 1) * HD]

    def turned(i):
        array, at, width, _ = spans[i]
        return jnp.concatenate([keys[array][r : r + HD, :] for r in range(at, at + width, HD)], axis=1)

    def with_ones(i):
        array, at, width, _ = spans[i]
        v = vals[array][at : at + width, :]
        return jnp.concatenate([v, jnp.ones((width, HD), v.dtype)], axis=1)

    def bias_of(base, width):
        key_pos = base + lax.broadcasted_iota(jnp.int32, (rows, width), 1)
        row_pos = row_base + lax.broadcasted_iota(jnp.int32, (rows, width), 0)
        starts = jnp.broadcast_to(start_ref[0].astype(jnp.float32), (HD, rows)).T
        starts = jnp.concatenate([starts] * (width // HD), axis=1)
        return jnp.where((key_pos <= row_pos) & (key_pos.astype(jnp.float32) >= starts), 0.0, NEG)

    def row_top(s):
        lane_top = s[:, :HD]
        for i in range(1, s.shape[1] // HD):
            lane_top = jnp.maximum(lane_top, s[:, i * HD : (i + 1) * HD])
        return jnp.max(lane_top, axis=1, keepdims=True)

    def weights_of(s, shift):
        wide = jnp.concatenate([shift] * (s.shape[1] // HD), axis=1)
        return jnp.exp2((s - wide) * EXP2_SCALE).astype(jnp.bfloat16)

    def step(kt, ve, base, mode, unroll):
        masked = base is not None
        if masked:
            bias = bias_of(base, kt.shape[1])

        def one_head(g, carry):
            q_here = q[g]
            s = jnp.dot(q_here, kt, preferred_element_type=jnp.float32)
            if masked:
                s = s + bias
            if mode == "first":
                m = jnp.broadcast_to(row_top(s), (rows, HD))
                top[h, t, g] = m
                acc[h, t, g] = jnp.dot(weights_of(s, m), ve, preferred_element_type=jnp.float32)
                sizes = jnp.abs(q_here.astype(jnp.float32))
                longest = jnp.maximum(carry[0], jnp.max(sizes.reshape(rows // 8, 8, HD), axis=0))
                lowest = jnp.minimum(carry[1], jnp.min(m.reshape(rows // 8, 8, HD), axis=0))
                return longest, lowest
            if mode == "kept":
                acc[h, t, g] += jnp.dot(weights_of(s, top[h, t, g]), ve, preferred_element_type=jnp.float32)
            else:
                m_old = top[h, t, g]
                m = jnp.maximum(m_old, row_top(s))
                fade = jnp.exp2((m_old - m) * EXP2_SCALE)
                update = jnp.dot(weights_of(s, m), ve, preferred_element_type=jnp.float32)
                top[h, t, g] = m
                acc[h, t, g] = acc[h, t, g] * jnp.concatenate([fade, fade], axis=1) + update
            return carry

        def some_heads(at, carry):
            for i in range(unroll):
                carry = one_head(at * unroll + i, carry)
            return carry

        carry = (jnp.zeros((8, HD), jnp.float32), jnp.full((8, HD), -NEG)) if mode == "first" else 0
        carry = lax.fori_loop(0, group // unroll, some_heads, carry)
        if mode == "first":
            reach[h, t, 0], reach[h, t, 1] = carry

    def all_keys(count):
        return jnp.concatenate([turned(i) for i in range(count)], axis=1)

    def all_values(count):
        return jnp.concatenate([with_ones(i) for i in range(count)], axis=0)

    count = len(spans)
    if first:
        pl.when(t == 0)(lambda: step(all_keys(1), all_values(1), bases[0], "first", group))
        pl.when(t == 1)(lambda: step(all_keys(count), all_values(count), bases[0], "first", group))
    else:
        room = jnp.min(reach[h, t, 1]) + SAFE / EXP2_SCALE
        widest = jnp.max(reach[h, t, 0], axis=0, keepdims=True)
        kt = all_keys(count).astype(jnp.float32)
        norms = jnp.max(jnp.sum(kt * kt, axis=0, keepdims=True), axis=1, keepdims=True)
        most = jnp.max(norms * jnp.sum(widest * widest, axis=1, keepdims=True)) * 1.01
        safe = (room > 0.0) & (most <= room * room)
        one_width = len({span[2] for span in spans}) == 1
        together = functools.reduce(jnp.logical_and, fulls) & safe if one_width else False
        if one_width:
            pl.when(together)(lambda: step(all_keys(count), all_values(count), None, "kept", group))

        def alone(chosen, width):
            def one_piece(piece, carry):
                choose = lambda options: functools.reduce(
                    lambda rest, i: jnp.where(piece == i, options[chosen[i]], rest),
                    range(1, len(chosen)),
                    options[chosen[0]],
                )
                base = choose(bases)
                run = choose([jnp.int32(r) for r in runs]) == 1

                @pl.when(run)
                def _():
                    for i, span in enumerate(chosen):

                        @pl.when(piece == i)
                        def _(span=span):
                            some_keys[:, :width] = turned(span)
                            some_values[:width] = with_ones(span)

                def part(base, mode, unroll):
                    return lambda: step(some_keys[:, :width], some_values[:width], base, mode, unroll)

                masked = run & safe
                if one_width:
                    full = choose([jnp.int32(f) for f in fulls]) == 1
                    pl.when(masked & full)(part(None, "kept", group))
                    masked = masked & jnp.logical_not(full)
                pl.when(masked)(part(base, "kept", group))
                pl.when(run & jnp.logical_not(safe))(part(base, "moved", 1))
                return carry

            lax.fori_loop(0, len(chosen), one_piece, 0)

        @pl.when(jnp.logical_not(together))
        def _():
            for width in sorted({span[2] for span in spans}):
                alone([i for i in range(count) if spans[i][2] == width], width)

    if fetch:
        pl.when((h == heads - 1) & (pl.program_id(1) == pl.num_programs(1) - 1))(copy.wait)
    if final:
        for g in range(group):
            a = acc[h, t, g]
            out_ref[:, g * HD : (g + 1) * HD] = (a[:, :HD] / a[:, HD:]).astype(jnp.bfloat16)


def attend(scalars, queries, got_queries, starts, pieces, spans, state, group, heads, which, weight=None, columns=0):
    rows, width = queries.shape[0], group * HD
    first, fetch, final = state is None, weight is not None, which != "both"
    tiles = 2 if which == "both" else 1

    def tile_of(t, ids):
        return {"both": t, "own": ids[0] % 2, "other": 1 - ids[0] % 2}[which]

    own_queries = (queries, pl.BlockSpec((rows, width), lambda h, t, *_: (0, h)))
    other_queries = (got_queries, pl.BlockSpec((rows, width), lambda h, t, *_: (0, h)))
    sources = {"both": [own_queries, other_queries], "own": [own_queries], "other": [other_queries]}[which]
    in_specs = [spec for _, spec in sources]
    in_specs.append(pl.BlockSpec((1, 1, rows), lambda h, t, i, *_: (tile_of(t, i), 0, 0)))
    in_specs += [pl.BlockSpec((p.shape[0], HD), lambda h, t, *_: (0, h)) for p in pieces]
    in_specs += [pl.BlockSpec((p.shape[0], HD), lambda h, t, *_: (0, heads + h)) for p in pieces]
    operands = [*scalars, *(array for array, _ in sources), starts, *pieces, *pieces]
    out_shape = [
        VMEM((heads, 2, group, rows, 2 * HD), jnp.float32),
        VMEM((heads, 2, group, rows, HD), jnp.float32),
        VMEM((heads, 2, 2, 8, HD), jnp.float32),
    ]
    aliases = {}
    if not first:
        out_shape = [VMEM(a.shape, a.dtype) for a in state]
        aliases = {len(operands) + i: i for i in range(len(state))}
        operands += state
        in_specs += [whole_vmem()] * len(state)
    out_specs = [whole_vmem()] * len(out_shape)
    wide = max(span[2] for span in spans)
    scratch = [
        VMEM((group, rows, HD), queries.dtype),
        VMEM((HD, wide), queries.dtype),
        VMEM((wide, 2 * HD), queries.dtype),
    ]
    if fetch:
        operands.append(weight)
        in_specs.append(pl.BlockSpec(memory_space=pl.ANY))
        out_shape.append(VMEM((weight.shape[0], columns), weight.dtype))
        out_specs.append(whole_vmem())
        scratch.append(pltpu.SemaphoreType.DMA)
    if final:
        out_shape.append(jax.ShapeDtypeStruct((rows, heads * width), queries.dtype))
        out_specs.append(pl.BlockSpec((rows, width), lambda h, t, *_: (0, h)))
    keys = sum(s[2] for s in spans)
    return pl.pallas_call(
        functools.partial(
            attend_body,
            q_count=len(sources),
            spans=spans,
            arrays=len(pieces),
            group=group,
            heads=heads,
            which=which,
            first=first,
            fetch=fetch,
            carried=0 if first else len(state),
            final=final,
        ),
        out_shape=out_shape,
        grid_spec=pltpu.PrefetchScalarGridSpec(
            num_scalar_prefetch=3,
            grid=(heads, tiles),
            in_specs=in_specs,
            out_specs=out_specs,
            scratch_shapes=scratch,
        ),
        input_output_aliases=aliases,
        compiler_params=pltpu.CompilerParams(vmem_limit_bytes=14 * MIB),
        cost_estimate=SMALL,
        name=f"attend_{which}_{keys}",
    )(*operands)


def project_held_body(ids, a_ref, b_ref, w_ref, alias, o_ref, *, at, tile):
    half = a_ref.shape[1]
    core = ids[0] % 2
    mine = pl.ds(pl.multiple_of(core * half, half), half)
    theirs = pl.ds(pl.multiple_of((1 - core) * half, half), half)
    for n in range(o_ref.shape[1] // tile):
        cols = slice(at + n * tile, at + (n + 1) * tile)
        total = jnp.dot(a_ref[...], w_ref[mine, cols], preferred_element_type=jnp.float32)
        total = total + jnp.dot(b_ref[...], w_ref[theirs, cols], preferred_element_type=jnp.float32)
        o_ref[:, n * tile : (n + 1) * tile] = total.astype(o_ref.dtype)


def project_held(ids, a, b, held, at, columns):
    rows, half = a.shape
    block = lambda shape: pl.BlockSpec(shape, lambda i, s: (0, 0))
    return pl.pallas_call(
        functools.partial(project_held_body, at=at, tile=min(256, columns)),
        out_shape=[VMEM(held.shape, held.dtype), jax.ShapeDtypeStruct((rows, columns), a.dtype)],
        grid_spec=pltpu.PrefetchScalarGridSpec(
            num_scalar_prefetch=1,
            grid=(1,),
            in_specs=[block((rows, half)), block((rows, half)), whole_vmem()],
            out_specs=[whole_vmem(), block((rows, columns))],
        ),
        input_output_aliases={3: 0},
        compiler_params=pltpu.CompilerParams(vmem_limit_bytes=16 * MIB),
        cost_estimate=pl.CostEstimate(flops=4 * rows * half * columns, bytes_accessed=64 * MIB, transcendentals=0),
        name="project_held",
    )(ids, a, b, held)


def project_body(ids, a_ref, b_ref, wa_ref, wb_ref, o_ref):
    total = jnp.dot(a_ref[...], wa_ref[...], preferred_element_type=jnp.float32)
    total = total + jnp.dot(b_ref[...], wb_ref[...], preferred_element_type=jnp.float32)
    o_ref[...] = total.astype(o_ref.dtype)


def project(ids, a, b, weight, columns, at, chosen, tile):
    rows, half = a.shape
    first = lambda s: (s[1] * columns + at) // tile
    block = pl.BlockSpec((rows, half), lambda n, s: (0, 0))
    return pl.pallas_call(
        project_body,
        out_shape=jax.ShapeDtypeStruct((rows, chosen), a.dtype),
        grid_spec=pltpu.PrefetchScalarGridSpec(
            num_scalar_prefetch=1,
            grid=(chosen // tile,),
            in_specs=[
                block,
                block,
                pl.BlockSpec((half, tile), lambda n, s: (s[0] % 2, first(s) + n)),
                pl.BlockSpec((half, tile), lambda n, s: (1 - s[0] % 2, first(s) + n)),
            ],
            out_specs=pl.BlockSpec((rows, tile), lambda n, s: (0, n)),
        ),
        compiler_params=pltpu.CompilerParams(vmem_limit_bytes=48 * MIB),
        cost_estimate=LARGE if at else SMALL,
        name="project",
    )(ids, a, b, weight, weight)


def add_body(kept, arrived, *refs):
    refs[-1][...] = (kept[...].astype(jnp.float32) + arrived[...].astype(jnp.float32)).astype(refs[-1].dtype)


def add_columns(kept, arrived, columns, at, before):
    rows, tile = kept.shape[0], 512
    block = pl.BlockSpec((rows, tile), lambda n: (0, n))
    return pl.pallas_call(
        add_body,
        out_shape=jax.ShapeDtypeStruct((rows, columns), kept.dtype),
        grid=(kept.shape[1] // tile,),
        in_specs=[block, block] + [pl.BlockSpec(memory_space=pl.ANY)] * len(before),
        out_specs=pl.BlockSpec((rows, tile), lambda n: (0, at // tile + n)),
        input_output_aliases={2: 0} if before else {},
        compiler_params=pltpu.CompilerParams(vmem_limit_bytes=8 * MIB),
        cost_estimate=SMALL,
        name="add_columns",
    )(kept, arrived, *before)


def on_device(queries, key_rows, values, lengths, block_plan, inverse, mask_lo, out_weight):
    rows, query_width = queries.shape
    kv_heads = key_rows.shape[1] // HD
    count, head_count = lax.axis_size("ctx"), lax.axis_size("head")
    here, head_here = lax.axis_index("ctx"), lax.axis_index("head")
    core = here % 2
    split = 2 if kv_heads % 2 == 0 else 1
    heads = kv_heads // split
    half = query_width // 2
    group = half // (heads * HD)
    levels = count // 8

    place = jnp.arange(3, dtype=jnp.int32)
    send_half = 1 - head_here if head_count == 2 else 0
    ids = jnp.where(place == 0, here, jnp.where(place == 1, head_here, send_half)).astype(jnp.int32)

    sibling = functools.partial(shift, count=count, partner=lambda i: i ^ 1)
    mine, send, kept_queries, sent_queries = pack(ids, key_rows, values, queries, split)
    swapped = sibling(send)
    lengths, mask_lo, _ = lax.optimization_barrier((lengths, mask_lo, send))
    chip_base = (here - core) * rows
    doc_ends = jnp.cumsum(lengths)
    pos = chip_base + jnp.arange(2 * rows, dtype=jnp.int32)
    doc_start = jnp.max(jnp.where(doc_ends[None, :] <= pos[:, None], doc_ends[None, :], 0), axis=1)
    low = lax.dynamic_slice_in_dim(mask_lo, chip_base // BLK, 2 * rows // BLK) * BLK
    starts = jnp.maximum(doc_start, jnp.repeat(low, BLK)).astype(jnp.int32).reshape(2, rows)
    scalars = (ids, jnp.min(starts, axis=1), jnp.max(starts, axis=1))
    start_rows = starts[:, None, :]
    swapped, start_rows, lows, highs = lax.optimization_barrier((swapped, start_rows, *scalars[1:]))
    scalars = (ids, lows, highs)

    up_level = functools.partial(shift, count=count, partner=lambda i: i + 4)
    first_hop = [up_level(mine), up_level(swapped)]
    own, upper = join(ids, mine, swapped)
    sent_queries, _ = lax.optimization_barrier((sent_queries, swapped))
    got_queries = sibling(sent_queries)

    common = (scalars, kept_queries, got_queries, start_rows)
    near = shift(own, count, lambda i: i + 2 if i // 2 % 2 == 0 else None)
    own_spans = [(0, 0, rows, lambda base, column, r: base), (0, rows, rows, lambda base, column, r: base + r)]
    state = attend(*common, [own], own_spans, None, group, heads, "both")
    keep = out_weight.shape[1] // head_count
    held_columns = keep if head_count == 2 else out_weight.shape[1]

    before, at_before = near, lambda base, column, r: jnp.where(column == 1, base - 2 * r, FAR)
    for d in range(1, levels + 1):
        if d == 1:
            first_hop = lax.optimization_barrier((*first_hop, state[2]))[:2]
            moving, _ = join(ids, *first_hop)
        else:
            moving, _ = lax.optimization_barrier((moving, state[2]))
        at_level = lambda base, column, r, d=d: base - 4 * d * r
        if d < levels:
            crossed = shift(moving, count, lambda i: i ^ 2)
            at_cross = lambda base, column, r, d=d: base - 4 * d * r + jnp.where(column == 0, 2 * r, -2 * r)
        else:
            crossed = shift(moving, count, lambda i: i - 2 if i // 2 % 2 == 1 else None)
            at_cross = lambda base, column, r, d=d: jnp.where(column == 0, base - 4 * d * r + 2 * r, FAR)
        onward = shift(moving, count, lambda i: i + 4) if d < levels else None
        if d == 1:
            reach = 4 * levels + 2
            upper, _ = lax.optimization_barrier((upper, moving))
            farthest = shift(upper, count, lambda i: i + reach)
        spans = [(0, 0, 2 * rows, at_before), (1, 0, 2 * rows, at_level)]
        fetch = (out_weight, held_columns) if d == 1 else ()
        state = attend(*common, [before, moving], spans, state, group, heads, "both", *fetch)
        before, at_before, moving = crossed, at_cross, onward
    at_farthest = lambda base, column, r: base - reach * r + r
    spans = [(0, 0, 2 * rows, at_before), (1, 0, rows, at_farthest)]
    *state, theirs = attend(*common, [before, farthest], spans, state, group, heads, "other")
    got = sibling(theirs)
    *state, att = attend(*common, [before, farthest], spans, state, group, heads, "own")
    held = state[3]

    if head_count != 2:
        _, partial_sums = project_held(ids, att, got, held, 0, held_columns)
        return lax.psum_scatter(partial_sums, "head", scatter_dimension=1, tiled=True)
    parts = ((0, keep // 4), (keep // 4, keep // 2), (3 * keep // 4, keep // 4))
    arrived = []
    for at, columns in parts:
        held, sent = project_held(ids, att, got, held, at, columns)
        arrived.append(lax.ppermute(sent, "head", [(0, 1), (1, 0)]))
    out = []
    for (at, columns), part in zip(parts, arrived):
        kept = project(ids, att, got, out_weight, keep, at, columns, 256)
        out = [add_columns(kept, part, keep, at, out)]
        ids, _ = lax.optimization_barrier((ids, out[0]))
    return out[0]


def solution(mesh):
    in_specs = (
        P("ctx", "head"),
        P("ctx", "head"),
        P("ctx", "head"),
        P(),
        P("ctx"),
        P(),
        P(),
        P("head", None),
    )
    return jax.shard_map(
        on_device, mesh=mesh, in_specs=in_specs, out_specs=P("ctx", "head"), check_vma=False
    )
```
